256 devices in a mesh: dp: 16 (over y_hi, x, core), seq: 16 (over y_lo, z).
Axes of the slice: x: 4, y: 4 (y_hi: 2, y_lo: 2; y = y_hi * 2 + y_lo), z: 8, core: 2. Of those that a mesh axis runs over, the one named last changes fastest.
Arguments:
- inputs: bfloat16 [16, 64, 256, 768], P('dp', 'seq'), may hold values from -6 to 6
- cotangent: bfloat16 [16, 64, 256, 768], P('dp', 'seq'), may hold values from -6 to 6
- value_weight: bfloat16 [768, 768], replicated, may hold values from -0.21875 to 0.21875
- up_weight: bfloat16 [768, 1536], replicated, may hold values from -0.21875 to 0.21875
- down_weight: bfloat16 [1536, 768], replicated, may hold values from -0.15625 to 0.15625
- first_blocks: bfloat16 [64, 256, 256], P('seq'), may hold values from -0.375 to 0.375
- second_blocks: bfloat16 [256, 64, 64], P('seq'), may hold values from -0.75 to 0.75
Outputs:
- value_grad: bfloat16 [768, 768], P('seq')
- up_grad: bfloat16 [768, 1536], P('seq')
- down_grad: bfloat16 [1536, 768], P('seq')
The draws below stay inside these ranges and needn't reach their ends.
All inputs are finite; a program needn't handle non-finite values.
Results may differ from the reference program's by a relative error of at most 0.02.
Values may be sent and summed in bfloat16 or wider, within the bound.
No kernel may reach another device: no remote copies, remote signals or barrier semaphores. Data moves between devices by JAX's collectives and lax.ppermute only.
A program may use at most 128 MiB of HBM per device.

```python
import jax
import jax.numpy as jnp
from jax import lax

D = 768
FF = 1536
M2 = 256
M1 = 64
BATCH = 16
TOKENS = 262144


def spiked(entries, key, source, target, shards_of, factor):
    def block_of(axis_at):
        return (jnp.arange(entries.shape[axis_at]) // (entries.shape[axis_at] // shards_of)).reshape((-1,) + (1,) * (entries.ndim - 1 - axis_at))

    near = jax.random.permutation(key, shards_of)[block_of(target)]
    other_side = (block_of(target) + shards_of // 2) % shards_of
    return jnp.where((block_of(source) == near) | (block_of(source) == other_side), factor * entries, entries)


def level_of(rng, shape, split, smallest, largest):
    gain = 1.0
    for position, parts in split:
        heights = jax.random.uniform(jax.random.fold_in(jax.random.fold_in(rng, 6), position), (parts,), jnp.float32, smallest / len(split), largest / len(split))
        gain = gain * jnp.repeat(jnp.exp(heights), shape[position] // parts).reshape((-1,) + (1,) * (len(shape) - 1 - position))
    return gain


def gaussian(own_key, dims, spread, limit, shards=(), kind=jnp.bfloat16):
    result = jax.random.normal(own_key, dims, jnp.float32) * spread
    if len(shards) > 0:
        result = level_of(own_key, dims, shards, -0.22, 0.18) * result
    return jnp.clip(result, min=-limit, max=limit).astype(kind)


def noise_with(rng, dims, width, reach, shards, heavy, dtype=jnp.bfloat16):
    result = width * jax.random.normal(rng, dims, jnp.float32)
    if shards:
        result = result * level_of(rng, dims, shards, -0.22, 0.18)
    return jnp.clip(spiked(result, jax.random.fold_in(rng, 3), *heavy), -reach, reach).astype(dtype)


def setup_inputs(seed: int = 0) -> dict:
    streams_of = jax.random.split(jax.random.key(seed), 8)
    return {
        "inputs": noise_with(streams_of[0], (BATCH, M1, M2, D), 1.0, 6.0, ((0, 16), (1, 16)), (1, 3, 16, 2.0)),
        "cotangent": noise_with(streams_of[1], (BATCH, M1, M2, D), 1.0, 6.0, ((0, 16), (1, 16)), (0, 3, 16, 2.0)),
        "value_weight": gaussian(streams_of[2], (D, D), D ** -0.5, 0.21875),
        "up_weight": gaussian(streams_of[3], (D, FF), D ** -0.5, 0.21875),
        "down_weight": gaussian(streams_of[4], (FF, D), FF ** -0.5, 0.15625),
        "first_blocks": gaussian(streams_of[5], (M1, M2, M2), M2 ** -0.5, 0.375, ((0, 16),)),
        "second_blocks": gaussian(streams_of[6], (M2, M1, M1), M1 ** -0.5, 0.75, ((0, 16),)),
    }


def gelu_tanh(field):
    return jax.nn.gelu(field, approximate=True)

def silu_slope(field):
    sigmoid_part = jax.nn.sigmoid(field)
    return sigmoid_part * (1.0 + field * (1.0 - sigmoid_part))

def reference(inputs, cotangent, value_weight, up_weight, down_weight, first_blocks, second_blocks):
    first_wide = first_blocks.astype(jnp.float32)
    second_wide = second_blocks.astype(jnp.float32)

    def one_document(carry, pair):
        source, slope_out = pair
        wide = source.astype(jnp.float32)
        normed = (wide * lax.rsqrt(lax.optimization_barrier(jnp.mean(wide * wide, axis=-1, keepdims=True)) + 1e-06)).astype(jnp.bfloat16)
        flat_normed = normed.reshape(-1, D)
        flat_cot = slope_out.reshape(-1, D)
        values = jnp.dot(flat_normed, value_weight, preferred_element_type=jnp.float32).astype(jnp.bfloat16)
        values = values.reshape(normed.shape)
        rowmix = jnp.einsum('acb,abd->acd', first_wide, values.astype(jnp.float32)).astype(jnp.bfloat16)
        mixed = jnp.einsum('cxy,ycd->xcd', second_wide, rowmix.astype(jnp.float32)).astype(jnp.bfloat16)
        slope = (slope_out.astype(jnp.float32) * normed.astype(jnp.float32) * silu_slope(mixed.astype(jnp.float32))).astype(jnp.bfloat16)
        back_rows = jnp.einsum('cxy,xcd->ycd', second_wide, slope.astype(jnp.float32)).astype(jnp.bfloat16)
        value_slope = jnp.einsum('acb,acd->abd', first_wide, back_rows.astype(jnp.float32)).astype(jnp.bfloat16)
        pre_act = jnp.dot(flat_normed, up_weight, preferred_element_type=jnp.float32)
        hidden = gelu_tanh(pre_act).astype(jnp.bfloat16)
        back_hidden = jnp.dot(flat_cot, down_weight.T, preferred_element_type=jnp.float32)
        up_slope = jax.vjp(gelu_tanh, pre_act)[1](back_hidden)[0].astype(jnp.bfloat16)
        grad_value = jnp.dot(flat_normed.T, value_slope.reshape(-1, D), preferred_element_type=jnp.float32)
        grad_up = jnp.dot(flat_normed.T, up_slope, preferred_element_type=jnp.float32)
        grad_down = jnp.dot(hidden.T, flat_cot, preferred_element_type=jnp.float32)
        return ((carry[0] + grad_value, carry[1] + grad_up, carry[2] + grad_down), None)
    start = (jnp.zeros((D, D), jnp.float32), jnp.zeros((D, FF), jnp.float32), jnp.zeros((FF, D), jnp.float32))
    totals, _ = lax.scan(one_document, start, (inputs, cotangent))
    factor = float(TOKENS) ** (-0.5)
    return ((totals[0] * factor).astype(jnp.bfloat16), (totals[1] * factor).astype(jnp.bfloat16), (totals[2] * factor).astype(jnp.bfloat16))
```

```python
import jax
import jax.numpy as jnp
from jax import lax
from jax.sharding import PartitionSpec as P

BF16 = jnp.bfloat16
F32 = jnp.float32
PIECE = [
    (i & 1) * 8 + ((((i >> 1) ^ (i >> 2)) & 1) * 4) + ((i >> 2) & 1) * 2 + (i >> 3)
    for i in range(16)
]
OWNER = [PIECE.index(p) for p in range(16)]


def gelu_tanh(field):
    return jax.nn.gelu(field, approximate=True)


def silu_slope(field):
    sigmoid_part = jax.nn.sigmoid(field)
    return sigmoid_part * (1.0 + field * (1.0 - sigmoid_part))


def product(left, right, left_dim, right_dim):
    return lax.dot_general(
        left, right, (((left_dim,), (right_dim,)), ((), ())), preferred_element_type=F32
    )


def swap(block, flip):
    return lax.ppermute(block, "dp", [(i, i ^ flip) for i in range(16)])


def halve(total, axis, bit, flip):
    mine = lax.dynamic_slice_in_dim(total, bit, 1, axis)
    other = lax.dynamic_slice_in_dim(total, 1 - bit, 1, axis).astype(BF16)
    return mine.astype(F32) + swap(other, flip).astype(F32)


def scatter_dp(left, right):
    i = lax.axis_index("dp")
    core, x0, x1, y_hi = i & 1, (i >> 1) & 1, (i >> 2) & 1, i >> 3
    out = []
    for first, block in ((True, left), (False, right)):
        rows, lanes = block.shape
        total = block.reshape(2, 2, 2, 2, rows // 16, lanes)
        total = halve(total, 0, core, 1)
        if first:
            total = halve(total, 1, x0 ^ x1, 2)
            total = halve(total, 2, x1, 6)
        else:
            total = halve(total, 2, x1, 6)
            total = halve(total, 1, x0 ^ x1, 2)
        total = halve(total, 3, y_hi, 8)
        out.append(total.reshape(rows // 16, lanes))
    return out


def exchange(block, axis):
    return lax.all_to_all(block, axis, split_axis=0, concat_axis=0, tiled=True)


def local(inputs, cotangent, value_weight, up_weight, down_weight, first_blocks, second_blocks):
    width = inputs.shape[3]
    rows = inputs.shape[1]
    places = lax.axis_size("seq")
    wide = inputs[0].astype(F32)
    normed = (wide * lax.rsqrt(jnp.mean(wide * wide, axis=-1, keepdims=True) + 1e-06)).astype(BF16)
    weighted = (cotangent[0].astype(F32) * normed.astype(F32)).astype(BF16)
    first_mix = jnp.einsum(
        "acb,abd->acd", first_blocks, normed, preferred_element_type=F32
    ).astype(BF16)

    def by_place(block):
        block = block.reshape(rows, places, -1, width).transpose(1, 0, 2, 3)
        return block.reshape(places, -1, width)

    sent = jnp.concatenate([by_place(first_mix), by_place(weighted)], axis=1)
    came = exchange(sent, "seq")
    half = came.shape[1] // 2
    first_mix = came[:, :half].reshape(-1, width)
    weighted = came[:, half:].reshape(-1, width)

    flat_normed = normed.reshape(-1, width)
    flat_cot = cotangent.reshape(-1, width)
    pre_act = product(flat_normed, up_weight, 1, 0)
    hidden = gelu_tanh(pre_act).astype(BF16)
    back_hidden = product(flat_cot, down_weight, 1, 1)
    up_slope = jax.vjp(gelu_tanh, pre_act)[1](back_hidden)[0].astype(BF16)
    up_t = product(up_slope, flat_normed, 0, 0).astype(BF16)
    down_t = product(flat_cot, hidden, 0, 0).astype(BF16)
    up_t, down_t = scatter_dp(up_t, down_t)

    blocks, size = second_blocks.shape[0], second_blocks.shape[1]
    positions = blocks * size
    stacked = second_blocks.transpose(1, 0, 2).reshape(positions, size)
    row = lax.broadcasted_iota(jnp.int32, (positions, positions), 0)
    col = lax.broadcasted_iota(jnp.int32, (positions, positions), 1)
    spread = (
        lax.broadcasted_iota(jnp.int32, (size, positions), 1) // blocks
        == lax.broadcasted_iota(jnp.int32, (size, positions), 0)
    ).astype(BF16)
    second = jnp.where(
        row % blocks == col % blocks, product(stacked, spread, 1, 0), 0.0
    ).astype(BF16)

    mix = product(second, first_mix, 1, 0).astype(BF16)
    mixed = product(mix, value_weight, 1, 0)
    slope = (weighted.astype(F32) * silu_slope(mixed)).astype(BF16)
    value_t = product(slope, mix, 0, 0).astype(BF16)
    value_left, value_right = scatter_dp(value_t[:, : width // 2], value_t[:, width // 2 :])
    value_t = jnp.concatenate([value_left, value_right], axis=1)

    piece_v, piece_u = value_t.shape[0], up_t.shape[0]
    value_p = value_t.astype(BF16).T.reshape(places, -1, piece_v)
    up_p = up_t.astype(BF16).T.reshape(places, -1, piece_u)
    down_p = down_t.astype(BF16).T.reshape(places, 2, -1, piece_v)
    packed = jnp.concatenate([value_p, up_p, down_p[:, 0], down_p[:, 1]], axis=2)
    total_tokens = (
        inputs.shape[0] * inputs.shape[1] * inputs.shape[2] * lax.axis_size("dp") * places
    )
    factor = float(total_tokens) ** (-0.5)
    packed = jnp.sum(exchange(packed, "seq").astype(F32), axis=0) * factor
    packed = packed.astype(BF16)
    packed = exchange(jnp.broadcast_to(packed[None], (16,) + packed.shape), "dp")
    packed = [packed[k] for k in OWNER]

    def join(start, size):
        return jnp.concatenate([block[:, start : start + size] for block in packed], axis=1)

    a, b = piece_v, piece_v + piece_u
    down = jnp.concatenate([join(b, piece_v), join(b + piece_v, piece_v)], axis=0)
    return join(0, a), join(a, piece_u), down


def solution(mesh):
    placed = (
        P("dp", "seq", None, None),
        P("dp", "seq", None, None),
        P(),
        P(),
        P(),
        P("seq", None, None),
        P("seq", None, None),
    )
    return jax.shard_map(
        local,
        mesh=mesh,
        in_specs=placed,
        out_specs=(P("seq", None), P("seq", None), P("seq", None)),
        check_vma=False,
    )
```

```python
import functools

import jax
import jax.numpy as jnp
from jax import lax
from jax.experimental import pallas as pl
from jax.experimental.pallas import tpu as pltpu
from jax.sharding import PartitionSpec as P

BF16 = jnp.bfloat16
F32 = jnp.float32
VMEM_LIMIT = 56 * 1024 * 1024
PIECE = [
    (i & 1) * 8 + ((((i >> 1) ^ (i >> 2)) & 1) * 4) + ((i >> 2) & 1) * 2 + (i >> 3)
    for i in range(16)
]


def product(left, right, left_dim, right_dim):
    return lax.dot_general(
        left, right, (((left_dim,), (right_dim,)), ((), ())), preferred_element_type=F32
    )


def normalise(block):
    wide = block.astype(F32)
    return (wide * lax.rsqrt(jnp.mean(wide * wide, axis=-1, keepdims=True) + 1e-06)).astype(BF16)


def send_kernel(inputs_ref, cot_ref, first_ref, sent_ref):
    normed = normalise(inputs_ref[0, 0])
    weighted = (cot_ref[0, 0].astype(F32) * normed.astype(F32)).astype(BF16)
    places, _, _, size, width = sent_ref.shape
    sent_ref[:, 1, 0] = weighted.reshape(places, size, width)
    mix = product(first_ref[0], normed, 1, 0).astype(BF16)
    sent_ref[:, 0, 0] = mix.reshape(places, size, width)


def build_sent(inputs, cotangent, first_blocks, places):
    _, rows, block, width = inputs.shape
    size = block // places
    whole = pl.BlockSpec((1, 1, block, width), lambda a: (0, a, 0, 0))
    return pl.pallas_call(
        send_kernel,
        grid=(rows,),
        in_specs=[whole, whole, pl.BlockSpec((1, block, block), lambda a: (a, 0, 0))],
        out_specs=pl.BlockSpec((places, 2, 1, size, width), lambda a: (0, 0, a, 0, 0)),
        out_shape=jax.ShapeDtypeStruct((places, 2, rows, size, width), BF16),
        compiler_params=pltpu.CompilerParams(vmem_limit_bytes=VMEM_LIMIT),
        name="send",
    )(inputs, cotangent, first_blocks)


def mlp_kernel(inputs_ref, cot_ref, up_ref, down_ref, up_t_ref, down_t_ref, normed_ref, cot_t_ref):
    @pl.when(pl.program_id(0) == 0)
    def _():
        normed_ref[...] = normalise(inputs_ref[...])
        cot_t_ref[...] = cot_ref[...].T

    field = product(normed_ref[...], up_ref[...], 1, 0)
    back = product(cot_ref[...], down_ref[...], 1, 1)
    scale, cubic = 0.7978845608028654, 0.044715
    square = field * field
    bend = jnp.tanh(scale * field * (1.0 + cubic * square))
    upper = 0.5 + 0.5 * bend
    hidden = (field * upper).astype(BF16)
    slope = upper + (0.5 * scale) * field * (1.0 - bend * bend) * (1.0 + 3.0 * cubic * square)
    up_slope = (back * slope).astype(BF16)
    down_t_ref[...] = product(cot_t_ref[...], hidden, 1, 0).astype(BF16)
    up_t_ref[...] = product(up_slope, normed_ref[...], 0, 0).astype(BF16)


def mlp_grads(inputs, cotangent, up_weight, down_weight):
    positions, width = inputs.shape
    units = up_weight.shape[1]
    step = 256
    whole = pl.BlockSpec((positions, width), lambda f: (0, 0))
    by_row = pl.BlockSpec((step, width), lambda f: (f, 0))
    by_col = pl.BlockSpec((width, step), lambda f: (0, f))
    return pl.pallas_call(
        mlp_kernel,
        grid=(units // step,),
        in_specs=[whole, whole, by_col, by_row],
        out_specs=[by_row, by_col],
        out_shape=[
            jax.ShapeDtypeStruct((units, width), BF16),
            jax.ShapeDtypeStruct((width, units), BF16),
        ],
        scratch_shapes=[pltpu.VMEM((positions, width), BF16), pltpu.VMEM((width, positions), BF16)],
        compiler_params=pltpu.CompilerParams(vmem_limit_bytes=VMEM_LIMIT),
        name="mlp",
    )(inputs, cotangent, up_weight, down_weight)


def spread_kernel(blocks, stacked_ref, out_ref):
    positions, size = stacked_ref.shape
    take = lax.broadcasted_iota(jnp.int32, (size, positions), 1) // blocks
    spread = (take == lax.broadcasted_iota(jnp.int32, (size, positions), 0)).astype(BF16)
    wide = product(stacked_ref[...], spread, 1, 0)
    row = lax.broadcasted_iota(jnp.int32, (positions, positions), 0)
    col = lax.broadcasted_iota(jnp.int32, (positions, positions), 1)
    out_ref[...] = jnp.where(row % blocks == col % blocks, wide, 0.0).astype(BF16)


def spread_second(second_blocks):
    blocks, size, _ = second_blocks.shape
    positions = blocks * size
    stacked = second_blocks.transpose(1, 0, 2).reshape(positions, size)
    return pl.pallas_call(
        functools.partial(spread_kernel, blocks),
        out_shape=jax.ShapeDtypeStruct((positions, positions), BF16),
        compiler_params=pltpu.CompilerParams(vmem_limit_bytes=VMEM_LIMIT),
        name="spread",
    )(stacked)


def value_kernel(mix_ref, weighted_ref, second_ref, weight_ref, out_ref, both_ref):
    positions = second_ref.shape[0]

    @pl.when(pl.program_id(0) == 0)
    def _():
        first_mix = mix_ref[:, 0].reshape(positions, -1)
        both_ref[...] = product(second_ref[...], first_mix, 1, 0).astype(BF16)

    mixed = product(both_ref[...], weight_ref[...], 1, 0)
    sigmoid_part = 0.5 + 0.5 * jnp.tanh(0.5 * mixed)
    weighted = weighted_ref[:, 0].reshape(mixed.shape).astype(F32)
    slope = weighted * (sigmoid_part * (1.0 + mixed * (1.0 - sigmoid_part)))
    out_ref[...] = product(slope.astype(BF16), both_ref[...], 0, 0).astype(BF16)


def value_grad(came, second, value_weight):
    places, _, size, width = came.shape
    positions = places * size
    step = 256
    return pl.pallas_call(
        value_kernel,
        grid=(width // step,),
        in_specs=[
            pl.BlockSpec((places, 1, size, width), lambda e: (0, 0, 0, 0)),
            pl.BlockSpec((places, 1, size, step), lambda e: (0, 1, 0, e)),
            pl.BlockSpec((positions, positions), lambda e: (0, 0)),
            pl.BlockSpec((width, step), lambda e: (0, e)),
        ],
        out_specs=pl.BlockSpec((step, width), lambda e: (e, 0)),
        out_shape=jax.ShapeDtypeStruct((width, width), BF16),
        scratch_shapes=[pltpu.VMEM((positions, width), BF16)],
        compiler_params=pltpu.CompilerParams(vmem_limit_bytes=VMEM_LIMIT),
        name="value",
    )(came, came, second, value_weight)


def join_kernel(pieces_ref, value_ref, up_ref, down_ref, rows_ref):
    places, size, lanes = pieces_ref.shape
    for i in range(places):
        rows_ref[PIECE[i] * size : (PIECE[i] + 1) * size, :lanes] = pieces_ref[i]
    turned = rows_ref[...].T
    width = value_ref.shape[1]
    share = value_ref.shape[0]
    value_ref[...] = turned[:share]
    up_ref[:, :width] = turned[share : 2 * share]
    up_ref[:, width:] = turned[2 * share : 3 * share]
    down_ref[...] = turned[3 * share : 5 * share]


def join(pieces):
    places, size, lanes = pieces.shape
    width = places * size
    share = lanes // 5
    padded = -(-lanes // 128) * 128
    return pl.pallas_call(
        join_kernel,
        out_shape=[
            jax.ShapeDtypeStruct((share, width), BF16),
            jax.ShapeDtypeStruct((share, 2 * width), BF16),
            jax.ShapeDtypeStruct((2 * share, width), BF16),
        ],
        scratch_shapes=[pltpu.VMEM((width, padded), BF16)],
        compiler_params=pltpu.CompilerParams(vmem_limit_bytes=VMEM_LIMIT),
        name="join",
    )(pieces)


def swap(block, flip):
    return lax.ppermute(block, "dp", [(i, i ^ flip) for i in range(16)])


def halve(total, axis, bit, flip):
    mine = lax.dynamic_slice_in_dim(total, bit, 1, axis)
    other = lax.dynamic_slice_in_dim(total, 1 - bit, 1, axis).astype(BF16)
    return mine.astype(F32) + swap(other, flip).astype(F32)


def scatter_dp(left, right):
    i = lax.axis_index("dp")
    core, x0, x1, y_hi = i & 1, (i >> 1) & 1, (i >> 2) & 1, i >> 3
    out = []
    for straight, block in ((True, left), (False, right)):
        groups, rows, lanes = block.shape
        total = block.reshape(groups, 2, 2, 2, 2, rows // 16, lanes)
        total = halve(total, 1, core, 1)
        if straight:
            total = halve(total, 2, x0 ^ x1, 2)
            total = halve(total, 3, x1, 6)
        else:
            total = halve(total, 3, x1, 6)
            total = halve(total, 2, x0 ^ x1, 2)
        total = halve(total, 4, y_hi, 8)
        out.append(total.reshape(groups, rows // 16, lanes))
    return out


def exchange(block, axis):
    return lax.all_to_all(block, axis, split_axis=0, concat_axis=0, tiled=True)


def by_place(block, places):
    rows, lanes = block.shape
    return block.astype(BF16).reshape(rows, places, lanes // places).transpose(1, 0, 2)


def local(inputs, cotangent, value_weight, up_weight, down_weight, first_blocks, second_blocks):
    width = inputs.shape[3]
    places = lax.axis_size("seq")
    sent = build_sent(inputs, cotangent, first_blocks, places)
    came = exchange(sent.reshape(places, 2, -1, width), "seq")

    second = spread_second(second_blocks)
    flat, second = lax.optimization_barrier((inputs.reshape(-1, width), second))
    up_t, down_t = mlp_grads(flat, cotangent.reshape(-1, width), up_weight, down_weight)
    up_t, down_t = scatter_dp(up_t.reshape(2, width, width), down_t[None])

    value_t = value_grad(came, second, value_weight)
    value_left, value_right = scatter_dp(
        value_t[None, :, : width // 2], value_t[None, :, width // 2 :]
    )
    value_t = jnp.concatenate([value_left[0], value_right[0]], axis=1)

    packed = jnp.concatenate(
        [by_place(part, places) for part in (value_t, up_t[0], up_t[1], down_t[0])], axis=2
    )
    total_tokens = (
        inputs.shape[0] * inputs.shape[1] * inputs.shape[2] * lax.axis_size("dp") * places
    )
    factor = float(total_tokens) ** (-0.5)
    packed = (jnp.sum(exchange(packed, "seq").astype(F32), axis=0) * factor).astype(BF16)
    return tuple(join(exchange(jnp.broadcast_to(packed[None], (16,) + packed.shape), "dp")))


def solution(mesh):
    placed = (
        P("dp", "seq", None, None),
        P("dp", "seq", None, None),
        P(),
        P(),
        P(),
        P("seq", None, None),
        P("seq", None, None),
    )
    return jax.shard_map(
        local,
        mesh=mesh,
        in_specs=placed,
        out_specs=(P("seq", None), P("seq", None), P("seq", None)),
        check_vma=False,
    )
```

```python
import jax
import jax.numpy as jnp
from jax import lax
from jax.experimental import pallas as pl
from jax.experimental.pallas import tpu as pltpu
from jax.sharding import PartitionSpec as P

BF16 = jnp.bfloat16
F32 = jnp.float32
VMEM_LIMIT = 56 * 1024 * 1024


def product(left, right, left_dim, right_dim):
    return lax.dot_general(
        left, right, (((left_dim,), (right_dim,)), ((), ())), preferred_element_type=F32
    )


def normalise(block):
    wide = block.astype(F32)
    return (wide * lax.rsqrt(jnp.mean(wide * wide, axis=-1, keepdims=True) + 1e-06)).astype(BF16)


def send_kernel(inputs_ref, cot_ref, first_ref, sent_ref):
    places, _, groups, tile, width = sent_ref.shape

    def part(block):
        return block.reshape(places, groups, -1, width)

    mixes, weights = [], []
    for a in range(inputs_ref.shape[1]):
        normed = normalise(inputs_ref[0, a])
        weights.append(part(cot_ref[0, a].astype(F32) * normed.astype(F32)))
        mixes.append(part(product(first_ref[a], normed, 1, 0)))
    for k, parts in enumerate((mixes, weights)):
        sent_ref[:, k] = jnp.concatenate(parts, axis=2).astype(BF16)


def build_sent(inputs, cotangent, first_blocks, places):
    _, rows, block, width = inputs.shape
    groups, step = 2, 2
    tile = step * block // places // groups
    whole = pl.BlockSpec((1, step, block, width), lambda a: (0, a, 0, 0))
    return pl.pallas_call(
        send_kernel,
        grid=(rows // step,),
        in_specs=[whole, whole, pl.BlockSpec((step, block, block), lambda a: (a, 0, 0))],
        out_specs=pl.BlockSpec((places, 2, groups, tile, width), lambda a: (0, 0, 0, a, 0)),
        out_shape=jax.ShapeDtypeStruct((places, 2, groups, tile * rows // step, width), BF16),
        compiler_params=pltpu.CompilerParams(vmem_limit_bytes=VMEM_LIMIT),
        name="send",
    )(inputs, cotangent, first_blocks)


def mlp_kernel(
    core_ref, inputs_ref, cot_ref, up_ref, down_ref,
    up_keep_ref, up_give_ref, down_keep_ref, down_give_ref, normed_ref, normed_t_ref,
):
    core, step, steps = core_ref[0], pl.program_id(0), pl.num_programs(0)

    @pl.when(step == 0)
    def _():
        normed = normalise(inputs_ref[...])
        normed_ref[...] = normed
        normed_t_ref[...] = normed.T

    field = product(normed_ref[...], up_ref[...], 1, 0)
    back = product(cot_ref[...], down_ref[...], 1, 1)
    scale, cubic = 0.7978845608028654, 0.044715
    square = field * field
    bend = jnp.tanh(scale * field * (1.0 + cubic * square))
    upper = 0.5 + 0.5 * bend
    hidden = (field * upper).astype(BF16)
    slope = upper + (0.5 * scale) * field * (1.0 - bend * bend) * (1.0 + 3.0 * cubic * square)
    up_slope = (back * slope).astype(BF16)
    up_grad = product(normed_t_ref[...], up_slope, 1, 0).astype(BF16)

    @pl.when(step < steps // 2)
    def _():
        up_give_ref[...] = up_grad

    @pl.when(step >= steps // 2)
    def _():
        up_keep_ref[...] = up_grad

    half = down_keep_ref.shape[1]
    hidden_t = hidden.T
    keep = pl.ds(pl.multiple_of(core * half, half), half)
    give = pl.ds(pl.multiple_of((1 - core) * half, half), half)
    down_keep_ref[...] = product(hidden_t, cot_ref[:, keep], 1, 0).astype(BF16)
    down_give_ref[...] = product(hidden_t, cot_ref[:, give], 1, 0).astype(BF16)


def mlp_grads(core, inputs, cotangent, up_weight, down_weight):
    positions, width = inputs.shape
    units = up_weight.shape[1]
    block = 256
    steps = units // block
    half = steps // 2

    def unit(f, c):
        return jnp.where(f < half, (1 - c[0]) * half + f, c[0] * half + f - half)

    whole = pl.BlockSpec((positions, width), lambda f, c: (0, 0))
    down_half = pl.BlockSpec((block, width // 2), lambda f, c: (unit(f, c), 0))
    return pl.pallas_call(
        mlp_kernel,
        grid_spec=pltpu.PrefetchScalarGridSpec(
            num_scalar_prefetch=1,
            grid=(steps,),
            in_specs=[
                whole,
                whole,
                pl.BlockSpec((width, block), lambda f, c: (0, unit(f, c))),
                pl.BlockSpec((block, width), lambda f, c: (unit(f, c), 0)),
            ],
            out_specs=[
                pl.BlockSpec((width, block), lambda f, c: (0, jnp.maximum(f - half, 0))),
                pl.BlockSpec((width, block), lambda f, c: (0, jnp.minimum(f, half - 1))),
                down_half,
                down_half,
            ],
            scratch_shapes=[
                pltpu.VMEM((positions, width), BF16),
                pltpu.VMEM((width, positions), BF16),
            ],
        ),
        out_shape=[jax.ShapeDtypeStruct((width, units // 2), BF16)] * 2
        + [jax.ShapeDtypeStruct((units, width // 2), BF16)] * 2,
        compiler_params=pltpu.CompilerParams(vmem_limit_bytes=VMEM_LIMIT),
        name="mlp",
    )(core, inputs, cotangent, up_weight, down_weight)


def spread_kernel(stacked_ref, out_ref):
    groups, positions, size = stacked_ref.shape
    blocks = positions // size
    take = lax.broadcasted_iota(jnp.int32, (size, positions), 1) // blocks
    spread = (take == lax.broadcasted_iota(jnp.int32, (size, positions), 0)).astype(BF16)
    row = lax.broadcasted_iota(jnp.int32, (positions, positions), 0)
    col = lax.broadcasted_iota(jnp.int32, (positions, positions), 1)
    same = row % blocks == col % blocks
    for k in range(groups):
        wide = product(stacked_ref[k], spread, 1, 0)
        out_ref[k] = jnp.where(same, wide, 0.0).astype(BF16)


def spread_second(second_blocks, groups):
    blocks, size, _ = second_blocks.shape
    positions = blocks // groups * size
    stacked = second_blocks.reshape(groups, -1, size, size).transpose(0, 2, 1, 3)
    return pl.pallas_call(
        spread_kernel,
        out_shape=jax.ShapeDtypeStruct((groups, positions, positions), BF16),
        compiler_params=pltpu.CompilerParams(vmem_limit_bytes=VMEM_LIMIT),
        name="spread",
    )(stacked.reshape(groups, positions, size))


def value_kernel(
    core_ref, mix_ref, weighted_ref, second_ref, weight_ref, keep_ref, give_ref, both_ref, both_t_ref
):
    groups, positions, _ = second_ref.shape
    step = pl.program_id(0)

    @pl.when(step == 0)
    def _():
        for k in range(groups):
            first_mix = mix_ref[:, 0, k].reshape(positions, -1)
            both = product(second_ref[k], first_mix, 1, 0).astype(BF16)
            rows = pl.ds(k * positions, positions)
            both_ref[rows] = both
            both_t_ref[:, rows] = both.T

    slopes = []
    for k in range(groups):
        mixed = product(both_ref[pl.ds(k * positions, positions)], weight_ref[...], 1, 0)
        sigmoid_part = 0.5 + 0.5 * jnp.tanh(0.5 * mixed)
        weighted = weighted_ref[:, 0, k].reshape(mixed.shape).astype(F32)
        slope = weighted * (sigmoid_part * (1.0 + mixed * (1.0 - sigmoid_part)))
        slopes.append(slope.astype(BF16))
    grad = product(both_t_ref[...], jnp.concatenate(slopes, axis=0), 1, 0).astype(BF16)

    @pl.when(step == 0)
    def _():
        give_ref[...] = grad

    @pl.when(step == 1)
    def _():
        keep_ref[...] = grad


def value_grad(core, came, second, value_weight):
    places, _, groups, tile, width = came.shape
    positions = places * groups * tile
    half = width // 2

    def part(e, c):
        return jnp.where(e == 0, 1 - c[0], c[0])

    whole = pl.BlockSpec((width, half), lambda e, c: (0, 0))
    return pl.pallas_call(
        value_kernel,
        grid_spec=pltpu.PrefetchScalarGridSpec(
            num_scalar_prefetch=1,
            grid=(2,),
            in_specs=[
                pl.BlockSpec((places, 1, groups, tile, width), lambda e, c: (0, 0, 0, 0, 0)),
                pl.BlockSpec((places, 1, groups, tile, half), lambda e, c: (0, 1, 0, 0, part(e, c))),
                pl.BlockSpec(second.shape, lambda e, c: (0, 0, 0)),
                pl.BlockSpec((width, half), lambda e, c: (0, part(e, c))),
            ],
            out_specs=[whole, whole],
            scratch_shapes=[
                pltpu.VMEM((positions, width), BF16),
                pltpu.VMEM((width, positions), BF16),
            ],
        ),
        out_shape=[jax.ShapeDtypeStruct((width, half), BF16)] * 2,
        compiler_params=pltpu.CompilerParams(vmem_limit_bytes=VMEM_LIMIT),
        name="value",
    )(core, came, came, second, value_weight)


def join_kernel(blocks_ref, value_ref, up_ref, down_ref):
    count, _, half = blocks_ref.shape
    share = value_ref.shape[0]
    cut = share // 2
    for core in range(2):
        lanes = slice(core * half, (core + 1) * half)
        total = blocks_ref[core, cut:].astype(F32)
        for i in range(2 + core, count, 2):
            total = total + blocks_ref[i, cut:].astype(F32)
        value_ref[:, lanes] = total.astype(BF16)
        for x1 in range(2):
            for x0 in range(2):
                i = x1 * 4 + x0 * 2 + core
                f, g = x0 ^ x1, x1
                column = (core * 2 + f) * half
                up_ref[g * cut : (g + 1) * cut, column : column + half] = blocks_ref[i, :cut]
                row = f * share + g * cut
                down_ref[row : row + cut, lanes] = blocks_ref[8 + i, :cut]


def join(blocks):
    _, rows, half = blocks.shape
    share = rows * 2 // 3
    return pl.pallas_call(
        join_kernel,
        out_shape=[
            jax.ShapeDtypeStruct((share, 2 * half), BF16),
            jax.ShapeDtypeStruct((share, 4 * half), BF16),
            jax.ShapeDtypeStruct((2 * share, 2 * half), BF16),
        ],
        compiler_params=pltpu.CompilerParams(vmem_limit_bytes=VMEM_LIMIT),
        name="join",
    )(blocks)


def swap(block, flip):
    return lax.ppermute(block, "dp", [(i, i ^ flip) for i in range(16)])


def add_swapped(keep, give, flip):
    return keep.astype(F32) + swap(give, flip).astype(F32)


def halve(total, axis, bit, flip):
    keep = lax.dynamic_slice_in_dim(total, bit, 1, axis)
    give = lax.dynamic_slice_in_dim(total, 1 - bit, 1, axis).astype(BF16)
    return add_swapped(keep, give, flip)


def exchange(block, axis):
    return lax.all_to_all(block, axis, split_axis=0, concat_axis=0, tiled=True)


def local(inputs, cotangent, value_weight, up_weight, down_weight, first_blocks, second_blocks):
    width = inputs.shape[3]
    places = lax.axis_size("seq")
    share, half = width // places, width // 2
    i = lax.axis_index("dp")
    core, x0, x1, y_hi = i & 1, (i >> 1) & 1, (i >> 2) & 1, i >> 3
    core_arg = jnp.full((1,), core, jnp.int32)

    came = exchange(build_sent(inputs, cotangent, first_blocks, places), "seq")

    flat = inputs.reshape(-1, width)
    grads = mlp_grads(core_arg, flat, cotangent.reshape(-1, width), up_weight, down_weight)
    up_keep, up_give, down_keep, down_give = grads
    second = spread_second(second_blocks, 2)

    up = add_swapped(up_keep, up_give, 1).reshape(places, 2, share // 2, 2, half)
    down = add_swapped(down_keep, down_give, 1).reshape(places, 2, 2, share // 2, half)
    up = halve(halve(up, 3, x0 ^ x1, 2), 1, x1, 6)
    down = halve(halve(down, 2, x1, 6), 1, x0 ^ x1, 2)
    up = up.reshape(places, share // 2, half)
    down = down.reshape(places, share // 2, half)
    keep = jnp.where(y_hi == 0, up, down)
    give = jnp.where(y_hi == 0, down, up).astype(BF16)
    mlp_part = add_swapped(keep, give, 8).astype(BF16)

    value_keep, value_give = value_grad(core_arg, came, second, value_weight)
    value_part = add_swapped(value_keep, value_give, 1).astype(BF16).reshape(places, share, half)

    part = exchange(jnp.concatenate([mlp_part, value_part], axis=1), "seq")
    total_tokens = (
        inputs.shape[0] * inputs.shape[1] * inputs.shape[2] * lax.axis_size("dp") * places
    )
    factor = float(total_tokens) ** (-0.5)
    part = (jnp.sum(part.astype(F32), axis=0) * factor).astype(BF16)
    return tuple(join(exchange(jnp.broadcast_to(part[None], (16,) + part.shape), "dp")))


def solution(mesh):
    placed = (
        P("dp", "seq", None, None),
        P("dp", "seq", None, None),
        P(),
        P(),
        P(),
        P("seq", None, None),
        P("seq", None, None),
    )
    return jax.shard_map(
        local,
        mesh=mesh,
        in_specs=placed,
        out_specs=(P("seq", None), P("seq", None), P("seq", None)),
        check_vma=False,
    )
```

```python
import jax
import jax.numpy as jnp
from jax import lax
from jax.experimental import pallas as pl
from jax.experimental.pallas import tpu as pltpu
from jax.sharding import PartitionSpec as P

BF16 = jnp.bfloat16
F32 = jnp.float32
VMEM_LIMIT = 56 * 1024 * 1024
PIECE = [
    (i & 1) * 8 + ((((i >> 1) ^ (i >> 2)) & 1) * 4) + ((i >> 2) & 1) * 2 + (i >> 3)
    for i in range(16)
]


def product(left, right, left_dim, right_dim):
    return lax.dot_general(
        left, right, (((left_dim,), (right_dim,)), ((), ())), preferred_element_type=F32
    )


def normalise(block):
    wide = block.astype(F32)
    return (wide * lax.rsqrt(jnp.mean(wide * wide, axis=-1, keepdims=True) + 1e-06)).astype(BF16)


def send_kernel(inputs_ref, cot_ref, first_ref, sent_ref):
    places, _, groups, tile, width = sent_ref.shape

    def part(block):
        return block.reshape(places, groups, -1, width)

    mixes, weights = [], []
    for a in range(inputs_ref.shape[1]):
        normed = normalise(inputs_ref[0, a])
        weights.append(part(cot_ref[0, a].astype(F32) * normed.astype(F32)))
        mixes.append(part(product(first_ref[a], normed, 1, 0)))
    for k, parts in enumerate((mixes, weights)):
        sent_ref[:, k] = jnp.concatenate(parts, axis=2).astype(BF16)


def build_sent(inputs, cotangent, first_blocks, places):
    _, rows, block, width = inputs.shape
    groups, step = 2, 2
    tile = step * block // places // groups
    whole = pl.BlockSpec((1, step, block, width), lambda a: (0, a, 0, 0))
    return pl.pallas_call(
        send_kernel,
        grid=(rows // step,),
        in_specs=[whole, whole, pl.BlockSpec((step, block, block), lambda a: (a, 0, 0))],
        out_specs=pl.BlockSpec((places, 2, groups, tile, width), lambda a: (0, 0, 0, a, 0)),
        out_shape=jax.ShapeDtypeStruct((places, 2, groups, tile * rows // step, width), BF16),
        compiler_params=pltpu.CompilerParams(vmem_limit_bytes=VMEM_LIMIT),
        name="send",
    )(inputs, cotangent, first_blocks)


def mlp_kernel(inputs_ref, cot_ref, up_ref, down_ref, up_t_ref, down_t_ref, normed_ref, cot_t_ref):
    @pl.when(pl.program_id(0) == 0)
    def _():
        normed_ref[...] = normalise(inputs_ref[...])
        cot_t_ref[...] = cot_ref[...].T

    field = product(normed_ref[...], up_ref[...], 1, 0)
    back = product(cot_ref[...], down_ref[...], 1, 1)
    scale, cubic = 0.7978845608028654, 0.044715
    square = field * field
    bend = jnp.tanh(scale * field * (1.0 + cubic * square))
    upper = 0.5 + 0.5 * bend
    hidden = (field * upper).astype(BF16)
    slope = upper + (0.5 * scale) * field * (1.0 - bend * bend) * (1.0 + 3.0 * cubic * square)
    up_slope = (back * slope).astype(BF16)
    down_t_ref[...] = product(cot_t_ref[...], hidden, 1, 0).astype(BF16)
    up_t_ref[...] = product(up_slope, normed_ref[...], 0, 0).astype(BF16)


def mlp_grads(inputs, cotangent, up_weight, down_weight):
    positions, width = inputs.shape
    units = up_weight.shape[1]
    step = 256
    whole = pl.BlockSpec((positions, width), lambda f: (0, 0))
    by_row = pl.BlockSpec((step, width), lambda f: (f, 0))
    by_col = pl.BlockSpec((width, step), lambda f: (0, f))
    return pl.pallas_call(
        mlp_kernel,
        grid=(units // step,),
        in_specs=[whole, whole, by_col, by_row],
        out_specs=[by_row, by_col],
        out_shape=[
            jax.ShapeDtypeStruct((units, width), BF16),
            jax.ShapeDtypeStruct((width, units), BF16),
        ],
        scratch_shapes=[pltpu.VMEM((positions, width), BF16), pltpu.VMEM((width, positions), BF16)],
        compiler_params=pltpu.CompilerParams(vmem_limit_bytes=VMEM_LIMIT),
        name="mlp",
    )(inputs, cotangent, up_weight, down_weight)


def spread_kernel(stacked_ref, out_ref):
    groups, positions, size = stacked_ref.shape
    blocks = positions // size
    take = lax.broadcasted_iota(jnp.int32, (size, positions), 1) // blocks
    spread = (take == lax.broadcasted_iota(jnp.int32, (size, positions), 0)).astype(BF16)
    row = lax.broadcasted_iota(jnp.int32, (positions, positions), 0)
    col = lax.broadcasted_iota(jnp.int32, (positions, positions), 1)
    same = row % blocks == col % blocks
    for k in range(groups):
        wide = product(stacked_ref[k], spread, 1, 0)
        out_ref[k] = jnp.where(same, wide, 0.0).astype(BF16)


def spread_second(second_blocks, groups):
    blocks, size, _ = second_blocks.shape
    positions = blocks // groups * size
    stacked = second_blocks.reshape(groups, -1, size, size).transpose(0, 2, 1, 3)
    return pl.pallas_call(
        spread_kernel,
        out_shape=jax.ShapeDtypeStruct((groups, positions, positions), BF16),
        compiler_params=pltpu.CompilerParams(vmem_limit_bytes=VMEM_LIMIT),
        name="spread",
    )(stacked.reshape(groups, positions, size))


def value_kernel(
    core_ref, mix_ref, weighted_ref, second_ref, weight_ref, keep_ref, give_ref, both_ref
):
    groups, positions, _ = second_ref.shape
    step = pl.program_id(0)

    @pl.when(step == 0)
    def _():
        for k in range(groups):
            first_mix = mix_ref[:, 0, k].reshape(positions, -1)
            both = product(second_ref[k], first_mix, 1, 0)
            both_ref[pl.ds(k * positions, positions)] = both.astype(BF16)

    slopes = []
    for k in range(groups):
        mixed = product(both_ref[pl.ds(k * positions, positions)], weight_ref[...], 1, 0)
        sigmoid_part = 0.5 + 0.5 * jnp.tanh(0.5 * mixed)
        weighted = weighted_ref[:, 0, k].reshape(mixed.shape).astype(F32)
        slope = weighted * (sigmoid_part * (1.0 + mixed * (1.0 - sigmoid_part)))
        slopes.append(slope.astype(BF16))
    grad = product(jnp.concatenate(slopes, axis=0), both_ref[...], 0, 0).astype(BF16)

    @pl.when(step == 0)
    def _():
        give_ref[...] = grad

    @pl.when(step == 1)
    def _():
        keep_ref[...] = grad


def value_grad(core, came, second, value_weight):
    places, _, groups, tile, width = came.shape
    positions = places * groups * tile
    half = width // 2

    def part(e, c):
        return jnp.where(e == 0, 1 - c[0], c[0])

    whole = pl.BlockSpec((half, width), lambda e, c: (0, 0))
    return pl.pallas_call(
        value_kernel,
        grid_spec=pltpu.PrefetchScalarGridSpec(
            num_scalar_prefetch=1,
            grid=(2,),
            in_specs=[
                pl.BlockSpec((places, 1, groups, tile, width), lambda e, c: (0, 0, 0, 0, 0)),
                pl.BlockSpec((places, 1, groups, tile, half), lambda e, c: (0, 1, 0, 0, part(e, c))),
                pl.BlockSpec(second.shape, lambda e, c: (0, 0, 0)),
                pl.BlockSpec((width, half), lambda e, c: (0, part(e, c))),
            ],
            out_specs=[whole, whole],
            scratch_shapes=[pltpu.VMEM((positions, width), BF16)],
        ),
        out_shape=[jax.ShapeDtypeStruct((half, width), BF16)] * 2,
        compiler_params=pltpu.CompilerParams(vmem_limit_bytes=24 * 1024 * 1024),
        name="value",
    )(core, came, came, second, value_weight)


def join_kernel(pieces_ref, value_ref, up_ref, down_ref, rows_ref):
    places, size, lanes = pieces_ref.shape
    for i in range(places):
        rows_ref[PIECE[i] * size : (PIECE[i] + 1) * size, :lanes] = pieces_ref[i]
    turned = rows_ref[...].T
    width = value_ref.shape[1]
    share = value_ref.shape[0]
    value_ref[...] = turned[:share]
    up_ref[:, :width] = turned[share : 2 * share]
    up_ref[:, width:] = turned[2 * share : 3 * share]
    down_ref[...] = turned[3 * share : 5 * share]


def join(pieces):
    places, size, lanes = pieces.shape
    width = places * size
    share = lanes // 5
    padded = -(-lanes // 128) * 128
    return pl.pallas_call(
        join_kernel,
        out_shape=[
            jax.ShapeDtypeStruct((share, width), BF16),
            jax.ShapeDtypeStruct((share, 2 * width), BF16),
            jax.ShapeDtypeStruct((2 * share, width), BF16),
        ],
        scratch_shapes=[pltpu.VMEM((width, padded), BF16)],
        compiler_params=pltpu.CompilerParams(vmem_limit_bytes=VMEM_LIMIT),
        name="join",
    )(pieces)


def swap(block, flip):
    return lax.ppermute(block, "dp", [(i, i ^ flip) for i in range(16)])


def add_swapped(keep, give, flip):
    return keep.astype(F32) + swap(give.astype(BF16), flip).astype(F32)


def halve(total, axis, bit, flip):
    keep = lax.dynamic_slice_in_dim(total, bit, 1, axis)
    give = lax.dynamic_slice_in_dim(total, 1 - bit, 1, axis)
    return add_swapped(keep, give, flip)


def scatter_chips(left, right):
    i = lax.axis_index("dp")
    x0, x1, y_hi = (i >> 1) & 1, (i >> 2) & 1, i >> 3
    out = []
    for straight, block in ((True, left), (False, right)):
        groups, rows, lanes = block.shape
        total = block.reshape(groups, 2, 2, 2, rows // 8, lanes)
        if straight:
            total = halve(total, 1, x0 ^ x1, 2)
            total = halve(total, 2, x1, 6)
        else:
            total = halve(total, 2, x1, 6)
            total = halve(total, 1, x0 ^ x1, 2)
        total = halve(total, 3, y_hi, 8)
        out.append(total.reshape(groups, rows // 8, lanes).astype(BF16))
    return out


def exchange(block, axis):
    return lax.all_to_all(block, axis, split_axis=0, concat_axis=0, tiled=True)


def by_place(block, places):
    rows, lanes = block.shape
    return block.reshape(rows, places, lanes // places).transpose(1, 0, 2)


def local(inputs, cotangent, value_weight, up_weight, down_weight, first_blocks, second_blocks):
    width = inputs.shape[3]
    half = width // 2
    places = lax.axis_size("seq")
    core = lax.axis_index("dp") & 1
    core_arg = jnp.full((1,), core, jnp.int32)
    total_tokens = (
        inputs.shape[0] * inputs.shape[1] * inputs.shape[2] * lax.axis_size("dp") * places
    )
    factor = float(total_tokens) ** (-0.5)

    def pack(parts):
        return jnp.concatenate([by_place(part, places) for part in parts], axis=2)

    came = exchange(build_sent(inputs, cotangent, first_blocks, places), "seq")

    flat = inputs.reshape(-1, width)
    up_t, down_t = mlp_grads(flat, cotangent.reshape(-1, width), up_weight, down_weight)
    up_t = halve(up_t.reshape(2, 2, half, width), 1, core, 1).reshape(2, half, width)
    down_t = halve(down_t.reshape(1, 2, half, 2 * width), 1, core, 1).reshape(1, half, 2 * width)
    up_t, down_t = scatter_chips(up_t, down_t)

    mlp_part = pack((up_t[0], up_t[1], down_t[0]))

    second = spread_second(second_blocks, 2)
    came, mlp_part, second = lax.optimization_barrier((came, mlp_part, second))
    value_keep, value_give = value_grad(core_arg, came, second, value_weight)
    value_t = add_swapped(value_keep, value_give, 1)
    value_left, value_right = scatter_chips(value_t[None, :, :half], value_t[None, :, half:])
    value_t = jnp.concatenate([value_left[0], value_right[0]], axis=1)

    part = exchange(jnp.concatenate([pack((value_t,)), mlp_part], axis=2), "seq")
    part = (jnp.sum(part.astype(F32), axis=0) * factor).astype(BF16)
    return tuple(join(exchange(jnp.broadcast_to(part[None], (16,) + part.shape), "dp")))


def solution(mesh):
    placed = (
        P("dp", "seq", None, None),
        P("dp", "seq", None, None),
        P(),
        P(),
        P(),
        P("seq", None, None),
        P("seq", None, None),
    )
    return jax.shard_map(
        local,
        mesh=mesh,
        in_specs=placed,
        out_specs=(P("seq", None), P("seq", None), P("seq", None)),
        check_vma=False,
    )
```

```python
import jax
import jax.numpy as jnp
from jax import lax
from jax.experimental import pallas as pl
from jax.experimental.pallas import tpu as pltpu
from jax.sharding import PartitionSpec as P

BF16 = jnp.bfloat16
F32 = jnp.float32
VMEM_LIMIT = 56 * 1024 * 1024
SMALL_LIMIT = 24 * 1024 * 1024
CHIPS = 8
PIECE = [
    (i & 1) * 8 + ((((i >> 1) ^ (i >> 2)) & 1) * 4) + ((i >> 2) & 1) * 2 + (i >> 3)
    for i in range(16)
]


def product(left, right, left_dim, right_dim):
    return lax.dot_general(
        left, right, (((left_dim,), (right_dim,)), ((), ())), preferred_element_type=F32
    )


def normalise(block):
    wide = block.astype(F32)
    return (wide * lax.rsqrt(jnp.mean(wide * wide, axis=-1, keepdims=True) + 1e-06)).astype(BF16)


def send_kernel(inputs_ref, cot_ref, first_ref, sent_ref):
    places, _, groups, tile, width = sent_ref.shape

    def part(block):
        return block.reshape(places, groups, -1, width)

    mixes, weights = [], []
    for a in range(inputs_ref.shape[1]):
        normed = normalise(inputs_ref[0, a])
        weights.append(part(cot_ref[0, a].astype(F32) * normed.astype(F32)))
        mixes.append(part(product(first_ref[a], normed, 1, 0)))
    for k, parts in enumerate((mixes, weights)):
        sent_ref[:, k] = jnp.concatenate(parts, axis=2).astype(BF16)


def build_sent(inputs, cotangent, first_blocks, places):
    _, rows, block, width = inputs.shape
    groups, step = 2, 2
    tile = step * block // places // groups
    whole = pl.BlockSpec((1, step, block, width), lambda a: (0, a, 0, 0))
    return pl.pallas_call(
        send_kernel,
        grid=(rows // step,),
        in_specs=[whole, whole, pl.BlockSpec((step, block, block), lambda a: (a, 0, 0))],
        out_specs=pl.BlockSpec((places, 2, groups, tile, width), lambda a: (0, 0, 0, a, 0)),
        out_shape=jax.ShapeDtypeStruct((places, 2, groups, tile * rows // step, width), BF16),
        compiler_params=pltpu.CompilerParams(vmem_limit_bytes=VMEM_LIMIT),
        name="send",
    )(inputs, cotangent, first_blocks)


def mlp_kernel(inputs_ref, cot_ref, up_ref, down_ref, up_t_ref, down_t_ref, normed_ref, cot_t_ref):
    @pl.when(pl.program_id(0) == 0)
    def _():
        normed_ref[...] = normalise(inputs_ref[...])
        cot_t_ref[...] = cot_ref[...].T

    field = product(normed_ref[...], up_ref[...], 1, 0)
    back = product(cot_ref[...], down_ref[...], 1, 1)
    scale, cubic = 0.7978845608028654, 0.044715
    square = field * field
    bend = jnp.tanh(scale * field * (1.0 + cubic * square))
    upper = 0.5 + 0.5 * bend
    hidden = (field * upper).astype(BF16)
    slope = upper + (0.5 * scale) * field * (1.0 - bend * bend) * (1.0 + 3.0 * cubic * square)
    up_slope = (back * slope).astype(BF16)
    down_t_ref[...] = product(cot_t_ref[...], hidden, 1, 0).astype(BF16)
    up_t_ref[...] = product(up_slope, normed_ref[...], 0, 0).astype(BF16)


def mlp_grads(inputs, cotangent, up_weight, down_weight):
    positions, width = inputs.shape
    units = up_weight.shape[1]
    step = 256
    whole = pl.BlockSpec((positions, width), lambda f: (0, 0))
    by_row = pl.BlockSpec((step, width), lambda f: (f, 0))
    by_col = pl.BlockSpec((width, step), lambda f: (0, f))
    return pl.pallas_call(
        mlp_kernel,
        grid=(units // step,),
        in_specs=[whole, whole, by_col, by_row],
        out_specs=[by_row, by_col],
        out_shape=[
            jax.ShapeDtypeStruct((units, width), BF16),
            jax.ShapeDtypeStruct((width, units), BF16),
        ],
        scratch_shapes=[pltpu.VMEM((positions, width), BF16), pltpu.VMEM((width, positions), BF16)],
        compiler_params=pltpu.CompilerParams(vmem_limit_bytes=VMEM_LIMIT),
        name="mlp",
    )(inputs, cotangent, up_weight, down_weight)


def value_kernel(
    core_ref, mix_ref, weighted_ref, stacked_ref, weight_ref, keep_ref, give_ref,
    both_ref, held_ref, copied,
):
    groups, positions, size = stacked_ref.shape
    step = pl.program_id(0)
    half = held_ref.shape[2]

    def copy(k):
        part = jnp.where(k == 0, 1 - core_ref[0], core_ref[0])
        lanes = pl.ds(pl.multiple_of(part * half, half), half)
        return pltpu.make_async_copy(weight_ref.at[:, lanes], held_ref.at[k], copied.at[k])

    @pl.when(step == 0)
    def _():
        copy(0).start()
        copy(1).start()
        blocks = positions // size
        take = lax.broadcasted_iota(jnp.int32, (size, positions), 1) // blocks
        spread = (take == lax.broadcasted_iota(jnp.int32, (size, positions), 0)).astype(BF16)
        row = lax.broadcasted_iota(jnp.int32, (positions, positions), 0)
        col = lax.broadcasted_iota(jnp.int32, (positions, positions), 1)
        same = row % blocks == col % blocks
        for k in range(groups):
            wide = product(stacked_ref[k], spread, 1, 0)
            second = jnp.where(same, wide, 0.0).astype(BF16)
            first_mix = mix_ref[:, 0, k].reshape(positions, -1)
            both = product(second, first_mix, 1, 0)
            both_ref[pl.ds(k * positions, positions)] = both.astype(BF16)
        copy(0).wait()

    @pl.when(step == 1)
    def _():
        copy(1).wait()

    slopes = []
    for k in range(groups):
        mixed = product(both_ref[pl.ds(k * positions, positions)], held_ref[step], 1, 0)
        sigmoid_part = 0.5 + 0.5 * jnp.tanh(0.5 * mixed)
        weighted = weighted_ref[:, 0, k].reshape(mixed.shape).astype(F32)
        slope = weighted * (sigmoid_part * (1.0 + mixed * (1.0 - sigmoid_part)))
        slopes.append(slope.astype(BF16))
    grad = product(jnp.concatenate(slopes, axis=0), both_ref[...], 0, 0).astype(BF16)
    size = grad.shape[0] // CHIPS
    pieces = [PIECE[2 * chip] % CHIPS for chip in range(CHIPS)]
    grad = jnp.concatenate([grad[p * size : (p + 1) * size] for p in pieces], axis=0)

    @pl.when(step == 0)
    def _():
        give_ref[...] = grad

    @pl.when(step == 1)
    def _():
        keep_ref[...] = grad


def value_grad(core, came, second_blocks, value_weight):
    places, _, groups, tile, width = came.shape
    positions = places * groups * tile
    half = width // 2
    size = second_blocks.shape[1]
    stacked = second_blocks.reshape(groups, -1, size, size).transpose(0, 2, 1, 3)
    stacked = stacked.reshape(groups, positions // groups, size)

    def part(e, c):
        return jnp.where(e == 0, 1 - c[0], c[0])

    whole = pl.BlockSpec((half, width), lambda e, c: (0, 0))
    return pl.pallas_call(
        value_kernel,
        grid_spec=pltpu.PrefetchScalarGridSpec(
            num_scalar_prefetch=1,
            grid=(2,),
            in_specs=[
                pl.BlockSpec((places, 1, groups, tile, width), lambda e, c: (0, 0, 0, 0, 0)),
                pl.BlockSpec((places, 1, groups, tile, half), lambda e, c: (0, 1, 0, 0, part(e, c))),
                pl.BlockSpec(stacked.shape, lambda e, c: (0, 0, 0)),
                pl.BlockSpec(memory_space=pltpu.HBM),
            ],
            out_specs=[whole, whole],
            scratch_shapes=[
                pltpu.VMEM((positions, width), BF16),
                pltpu.VMEM((2, width, half), BF16),
                pltpu.SemaphoreType.DMA((2,)),
            ],
        ),
        out_shape=[jax.ShapeDtypeStruct((half, width), BF16)] * 2,
        compiler_params=pltpu.CompilerParams(vmem_limit_bytes=SMALL_LIMIT),
        name="value",
    )(core, came, came, stacked, value_weight)


def join_kernel(pieces_ref, value_ref, up_ref, down_ref, rows_ref):
    places, size, lanes = pieces_ref.shape
    for i in range(places):
        rows_ref[PIECE[i] * size : (PIECE[i] + 1) * size, :lanes] = pieces_ref[i]
    turned = rows_ref[...].T
    width = value_ref.shape[1]
    share = value_ref.shape[0]
    value_ref[...] = turned[:share]
    up_ref[:, :width] = turned[share : 2 * share]
    up_ref[:, width:] = turned[2 * share : 3 * share]
    down_ref[...] = turned[3 * share : 5 * share]


def join(pieces):
    places, size, lanes = pieces.shape
    width = places * size
    share = lanes // 5
    padded = -(-lanes // 128) * 128
    return pl.pallas_call(
        join_kernel,
        out_shape=[
            jax.ShapeDtypeStruct((share, width), BF16),
            jax.ShapeDtypeStruct((share, 2 * width), BF16),
            jax.ShapeDtypeStruct((2 * share, width), BF16),
        ],
        scratch_shapes=[pltpu.VMEM((width, padded), BF16)],
        compiler_params=pltpu.CompilerParams(vmem_limit_bytes=SMALL_LIMIT),
        name="join",
    )(pieces)


def swap(block, flip):
    return lax.ppermute(block, "dp", [(i, i ^ flip) for i in range(16)])


def add_swapped(keep, give, flip):
    return keep.astype(F32) + swap(give.astype(BF16), flip).astype(F32)


def halve(total, axis, bit, flip):
    keep = lax.dynamic_slice_in_dim(total, bit, 1, axis)
    give = lax.dynamic_slice_in_dim(total, 1 - bit, 1, axis)
    return add_swapped(keep, give, flip)


def scatter_chips(left, right):
    i = lax.axis_index("dp")
    x0, x1, y_hi = (i >> 1) & 1, (i >> 2) & 1, i >> 3
    out = []
    for straight, block in ((True, left), (False, right)):
        groups, rows, lanes = block.shape
        total = block.reshape(groups, 2, 2, 2, rows // 8, lanes)
        if straight:
            total = halve(total, 1, x0 ^ x1, 2)
            total = halve(total, 2, x1, 6)
        else:
            total = halve(total, 2, x1, 6)
            total = halve(total, 1, x0 ^ x1, 2)
        total = halve(total, 3, y_hi, 8)
        out.append(total.reshape(groups, rows // 8, lanes).astype(BF16))
    return out


def exchange(block, axis, groups=None):
    return lax.all_to_all(
        block, axis, split_axis=0, concat_axis=0, tiled=True, axis_index_groups=groups
    )


def same_core():
    return [[2 * chip + core for chip in range(CHIPS)] for core in range(2)]


def by_place(block, places):
    rows, lanes = block.shape
    return block.reshape(rows, places, lanes // places).transpose(1, 0, 2)


def local(inputs, cotangent, value_weight, up_weight, down_weight, first_blocks, second_blocks):
    width = inputs.shape[3]
    half = width // 2
    places = lax.axis_size("seq")
    core = lax.axis_index("dp") & 1
    core_arg = jnp.full((1,), core, jnp.int32)
    total_tokens = (
        inputs.shape[0] * inputs.shape[1] * inputs.shape[2] * lax.axis_size("dp") * places
    )
    factor = float(total_tokens) ** (-0.5)

    def pack(parts):
        return jnp.concatenate([by_place(part, places) for part in parts], axis=2)

    came = exchange(build_sent(inputs, cotangent, first_blocks, places), "seq")

    flat = inputs.reshape(-1, width)
    up_t, down_t = mlp_grads(flat, cotangent.reshape(-1, width), up_weight, down_weight)
    up_t = halve(up_t.reshape(2, 2, half, width), 1, core, 1).reshape(2, half, width)
    down_t = halve(down_t.reshape(1, 2, half, 2 * width), 1, core, 1).reshape(1, half, 2 * width)
    up_t, down_t = scatter_chips(up_t, down_t)

    mlp_part = pack((up_t[0], up_t[1], down_t[0]))

    came, mlp_part = lax.optimization_barrier((came, mlp_part))
    value_keep, value_give = value_grad(core_arg, came, second_blocks, value_weight)
    value_t = add_swapped(value_keep, value_give, 1)
    value_t = exchange(value_t.astype(BF16).reshape(CHIPS, -1, width), "dp", same_core())
    value_t = jnp.sum(value_t.astype(F32), axis=0).astype(BF16)

    part = exchange(jnp.concatenate([pack((value_t,)), mlp_part], axis=2), "seq")
    part = (jnp.sum(part.astype(F32), axis=0) * factor).astype(BF16)
    return tuple(join(exchange(jnp.broadcast_to(part[None], (16,) + part.shape), "dp")))


def solution(mesh):
    placed = (
        P("dp", "seq", None, None),
        P("dp", "seq", None, None),
        P(),
        P(),
        P(),
        P("seq", None, None),
        P("seq", None, None),
    )
    return jax.shard_map(
        local,
        mesh=mesh,
        in_specs=placed,
        out_specs=(P("seq", None), P("seq", None), P("seq", None)),
        check_vma=False,
    )
```

```python
import jax
import jax.numpy as jnp
from jax import lax
from jax.experimental import pallas as pl
from jax.experimental.pallas import tpu as pltpu
from jax.sharding import PartitionSpec as P

BF16 = jnp.bfloat16
F32 = jnp.float32
VMEM_LIMIT = 56 * 1024 * 1024
SMALL_LIMIT = 24 * 1024 * 1024
CHIPS = 8
PIECE = [
    (i & 1) * 8 + ((((i >> 1) ^ (i >> 2)) & 1) * 4) + ((i >> 2) & 1) * 2 + (i >> 3)
    for i in range(16)
]


def product(left, right, left_dim, right_dim):
    return lax.dot_general(
        left, right, (((left_dim,), (right_dim,)), ((), ())), preferred_element_type=F32
    )


def normalise(block):
    wide = block.astype(F32)
    return (wide * lax.rsqrt(jnp.mean(wide * wide, axis=-1, keepdims=True) + 1e-06)).astype(BF16)


def send_kernel(inputs_ref, cot_ref, first_ref, sent_ref):
    places, _, groups, tile, width = sent_ref.shape

    def part(block):
        return block.reshape(places, groups, -1, width)

    mixes, weights = [], []
    for a in range(inputs_ref.shape[1]):
        normed = normalise(inputs_ref[0, a])
        weights.append(part(cot_ref[0, a].astype(F32) * normed.astype(F32)))
        mixes.append(part(product(first_ref[a], normed, 1, 0)))
    for k, parts in enumerate((mixes, weights)):
        sent_ref[:, k] = jnp.concatenate(parts, axis=2).astype(BF16)


def build_sent(inputs, cotangent, first_blocks, places):
    _, rows, block, width = inputs.shape
    groups, step = 2, 2
    tile = step * block // places // groups
    whole = pl.BlockSpec((1, step, block, width), lambda a: (0, a, 0, 0))
    return pl.pallas_call(
        send_kernel,
        grid=(rows // step,),
        in_specs=[whole, whole, pl.BlockSpec((step, block, block), lambda a: (a, 0, 0))],
        out_specs=pl.BlockSpec((places, 2, groups, tile, width), lambda a: (0, 0, 0, a, 0)),
        out_shape=jax.ShapeDtypeStruct((places, 2, groups, tile * rows // step, width), BF16),
        compiler_params=pltpu.CompilerParams(vmem_limit_bytes=VMEM_LIMIT),
        name="send",
    )(inputs, cotangent, first_blocks)


def mlp_kernel(inputs_ref, cot_ref, up_ref, down_ref, up_t_ref, down_t_ref, normed_ref, cot_t_ref):
    @pl.when(pl.program_id(0) == 0)
    def _():
        normed_ref[...] = normalise(inputs_ref[...])
        cot_t_ref[...] = cot_ref[...].T

    field = product(normed_ref[...], up_ref[...], 1, 0)
    back = product(cot_ref[...], down_ref[...], 1, 1)
    scale, cubic = 0.7978845608028654, 0.044715
    square = field * field
    bend = jnp.tanh(scale * field * (1.0 + cubic * square))
    upper = 0.5 + 0.5 * bend
    hidden = (field * upper).astype(BF16)
    slope = upper + (0.5 * scale) * field * (1.0 - bend * bend) * (1.0 + 3.0 * cubic * square)
    up_slope = (back * slope).astype(BF16)
    down_t_ref[...] = product(cot_t_ref[...], hidden, 1, 0).astype(BF16)
    up_t_ref[...] = product(up_slope, normed_ref[...], 0, 0).astype(BF16)


def mlp_grads(inputs, cotangent, up_weight, down_weight):
    positions, width = inputs.shape
    units = up_weight.shape[1]
    step = 256
    whole = pl.BlockSpec((positions, width), lambda f: (0, 0))
    by_row = pl.BlockSpec((step, width), lambda f: (f, 0))
    by_col = pl.BlockSpec((width, step), lambda f: (0, f))
    return pl.pallas_call(
        mlp_kernel,
        grid=(units // step,),
        in_specs=[whole, whole, by_col, by_row],
        out_specs=[by_row, by_col],
        out_shape=[
            jax.ShapeDtypeStruct((units, width), BF16),
            jax.ShapeDtypeStruct((width, units), BF16),
        ],
        scratch_shapes=[pltpu.VMEM((positions, width), BF16), pltpu.VMEM((width, positions), BF16)],
        compiler_params=pltpu.CompilerParams(vmem_limit_bytes=VMEM_LIMIT),
        name="mlp",
    )(inputs, cotangent, up_weight, down_weight)


def value_half(both_ref, weighted_ref, weight_ref, out_ref):
    slopes = []
    groups = weighted_ref.shape[2]
    positions = both_ref.shape[0] // groups
    for k in range(groups):
        mixed = product(both_ref[pl.ds(k * positions, positions)], weight_ref[...], 1, 0)
        sigmoid_part = 0.5 + 0.5 * jnp.tanh(0.5 * mixed)
        weighted = weighted_ref[:, 0, k].reshape(mixed.shape).astype(F32)
        slope = weighted * (sigmoid_part * (1.0 + mixed * (1.0 - sigmoid_part)))
        slopes.append(slope.astype(BF16))
    grad = product(jnp.concatenate(slopes, axis=0), both_ref[...], 0, 0).astype(BF16)
    size = grad.shape[0] // CHIPS
    pieces = [PIECE[2 * chip] % CHIPS for chip in range(CHIPS)]
    out_ref[...] = jnp.concatenate([grad[p * size : (p + 1) * size] for p in pieces], axis=0)


def give_kernel(part_ref, mix_ref, weighted_ref, stacked_ref, weight_ref, both_ref, out_ref):
    groups, positions, size = stacked_ref.shape
    blocks = positions // size
    take = lax.broadcasted_iota(jnp.int32, (size, positions), 1) // blocks
    spread = (take == lax.broadcasted_iota(jnp.int32, (size, positions), 0)).astype(BF16)
    row = lax.broadcasted_iota(jnp.int32, (positions, positions), 0)
    col = lax.broadcasted_iota(jnp.int32, (positions, positions), 1)
    same = row % blocks == col % blocks
    for k in range(groups):
        wide = product(stacked_ref[k], spread, 1, 0)
        second = jnp.where(same, wide, 0.0).astype(BF16)
        first_mix = mix_ref[:, 0, k].reshape(positions, -1)
        both_ref[pl.ds(k * positions, positions)] = product(second, first_mix, 1, 0).astype(BF16)
    value_half(both_ref, weighted_ref, weight_ref, out_ref)


def keep_kernel(part_ref, both_ref, weighted_ref, weight_ref, out_ref):
    value_half(both_ref, weighted_ref, weight_ref, out_ref)


def value_specs(came):
    places, _, groups, tile, width = came.shape
    half = width // 2
    positions = places * groups * tile
    return (
        pl.BlockSpec((places, 1, groups, tile, width), lambda k, p: (0, 0, 0, 0, 0)),
        pl.BlockSpec((places, 1, groups, tile, half), lambda k, p: (0, 1, 0, 0, p[0])),
        pl.BlockSpec((positions, width), lambda k, p: (0, 0)),
        pl.BlockSpec((width, half), lambda k, p: (0, p[0])),
        pl.BlockSpec((half, width), lambda k, p: (0, 0)),
        jax.ShapeDtypeStruct((positions, width), BF16),
        jax.ShapeDtypeStruct((half, width), BF16),
    )


def value_given(part, came, second_blocks, value_weight):
    mix, weighted, both, weight, out, both_shape, out_shape = value_specs(came)
    groups, size = came.shape[2], second_blocks.shape[1]
    stacked = second_blocks.reshape(groups, -1, size, size).transpose(0, 2, 1, 3)
    stacked = stacked.reshape(groups, -1, size)
    return pl.pallas_call(
        give_kernel,
        grid_spec=pltpu.PrefetchScalarGridSpec(
            num_scalar_prefetch=1,
            grid=(1,),
            in_specs=[mix, weighted, pl.BlockSpec(stacked.shape, lambda k, p: (0, 0, 0)), weight],
            out_specs=[both, out],
        ),
        out_shape=[both_shape, out_shape],
        compiler_params=pltpu.CompilerParams(vmem_limit_bytes=SMALL_LIMIT),
        name="give",
    )(part, came, came, stacked, value_weight)


def value_kept(part, both, came, value_weight):
    _, weighted, rows, weight, out, _, out_shape = value_specs(came)
    return pl.pallas_call(
        keep_kernel,
        grid_spec=pltpu.PrefetchScalarGridSpec(
            num_scalar_prefetch=1,
            grid=(1,),
            in_specs=[rows, weighted, weight],
            out_specs=out,
        ),
        out_shape=out_shape,
        compiler_params=pltpu.CompilerParams(vmem_limit_bytes=SMALL_LIMIT),
        name="keep",
    )(part, both, came, value_weight)


def join_kernel(pieces_ref, value_ref, up_ref, down_ref, rows_ref):
    places, size, lanes = pieces_ref.shape
    for i in range(places):
        rows_ref[PIECE[i] * size : (PIECE[i] + 1) * size, :lanes] = pieces_ref[i]
    turned = rows_ref[...].T
    width = value_ref.shape[1]
    share = value_ref.shape[0]
    value_ref[...] = turned[:share]
    up_ref[:, :width] = turned[share : 2 * share]
    up_ref[:, width:] = turned[2 * share : 3 * share]
    down_ref[...] = turned[3 * share : 5 * share]


def join(pieces):
    places, size, lanes = pieces.shape
    width = places * size
    share = lanes // 5
    padded = -(-lanes // 128) * 128
    return pl.pallas_call(
        join_kernel,
        out_shape=[
            jax.ShapeDtypeStruct((share, width), BF16),
            jax.ShapeDtypeStruct((share, 2 * width), BF16),
            jax.ShapeDtypeStruct((2 * share, width), BF16),
        ],
        scratch_shapes=[pltpu.VMEM((width, padded), BF16)],
        compiler_params=pltpu.CompilerParams(vmem_limit_bytes=SMALL_LIMIT),
        name="join",
    )(pieces)


def swap(block, flip, over):
    return lax.ppermute(block, over, [(i, i ^ flip) for i in range(16)])


def add_swapped(keep, give, flip, over="dp"):
    return keep.astype(F32) + swap(give.astype(BF16), flip, over).astype(F32)


def halve(total, axis, bit, flip, over="dp"):
    keep = lax.dynamic_slice_in_dim(total, bit, 1, axis)
    give = lax.dynamic_slice_in_dim(total, 1 - bit, 1, axis)
    return add_swapped(keep, give, flip, over)


def scatter_chips(left, right):
    i = lax.axis_index("dp")
    x0, x1, y_hi = (i >> 1) & 1, (i >> 2) & 1, i >> 3
    out = []
    for straight, block in ((True, left), (False, right)):
        groups, rows, lanes = block.shape
        total = block.reshape(groups, 2, 2, 2, rows // 8, lanes)
        if straight:
            total = halve(total, 1, x0 ^ x1, 2)
            total = halve(total, 2, x1, 6)
        else:
            total = halve(total, 2, x1, 6)
            total = halve(total, 1, x0 ^ x1, 2)
        total = halve(total, 3, y_hi, 8)
        out.append(total.reshape(groups, rows // 8, lanes).astype(BF16))
    return out


def exchange(block, axis, groups=None):
    return lax.all_to_all(
        block, axis, split_axis=0, concat_axis=0, tiled=True, axis_index_groups=groups
    )


def same_core():
    return [[2 * chip + core for chip in range(CHIPS)] for core in range(2)]


def by_place(block, places):
    rows, lanes = block.shape
    return block.reshape(rows, places, lanes // places).transpose(1, 0, 2)


def local(inputs, cotangent, value_weight, up_weight, down_weight, first_blocks, second_blocks):
    width = inputs.shape[3]
    half = width // 2
    places = lax.axis_size("seq")
    share = width // places
    core = lax.axis_index("dp") & 1
    core_arg = jnp.full((1,), core, jnp.int32)
    total_tokens = (
        inputs.shape[0] * inputs.shape[1] * inputs.shape[2] * lax.axis_size("dp") * places
    )
    factor = float(total_tokens) ** (-0.5)

    def pack(parts):
        return jnp.concatenate([by_place(part, places) for part in parts], axis=2)

    came = exchange(build_sent(inputs, cotangent, first_blocks, places), "seq")

    flat = inputs.reshape(-1, width)
    up_t, down_t = mlp_grads(flat, cotangent.reshape(-1, width), up_weight, down_weight)
    up_t = halve(up_t.reshape(2, 2, half, width), 1, core, 1).reshape(2, half, width)
    down_t = halve(down_t.reshape(1, 2, half, 2 * width), 1, core, 1).reshape(1, half, 2 * width)
    up_t, down_t = scatter_chips(up_t, down_t)


    came, up_t, down_t = lax.optimization_barrier((came, up_t, down_t))
    both, value_give = value_given(1 - core_arg, came, second_blocks, value_weight)
    value_keep = value_kept(core_arg, both, came, value_weight)
    value_t = add_swapped(value_keep, value_give, 1).astype(BF16)

    value_t, up_t, down_t = lax.optimization_barrier((value_t, up_t, down_t))
    value_t = exchange(value_t.reshape(CHIPS, -1, width), "dp", same_core())
    mlp_part = pack((up_t[0], up_t[1], down_t[0]))
    value_t = jnp.sum(value_t.astype(F32), axis=0).astype(BF16)

    part = exchange(jnp.concatenate([pack((value_t,)), mlp_part], axis=2), "seq")
    part = (jnp.sum(part.astype(F32), axis=0) * factor).astype(BF16)
    return tuple(join(exchange(jnp.broadcast_to(part[None], (16,) + part.shape), "dp")))


def solution(mesh):
    placed = (
        P("dp", "seq", None, None),
        P("dp", "seq", None, None),
        P(),
        P(),
        P(),
        P("seq", None, None),
        P("seq", None, None),
    )
    return jax.shard_map(
        local,
        mesh=mesh,
        in_specs=placed,
        out_specs=(P("seq", None), P("seq", None), P("seq", None)),
        check_vma=False,
    )
```

```python
import jax
import jax.numpy as jnp
from jax import lax
from jax.experimental import pallas as pl
from jax.experimental.pallas import tpu as pltpu
from jax.sharding import PartitionSpec as P

BF16 = jnp.bfloat16
F32 = jnp.float32
VMEM_LIMIT = 56 * 1024 * 1024
SMALL_LIMIT = 24 * 1024 * 1024
CHIPS = 8
PIECE = [
    (i & 1) * 8 + ((((i >> 1) ^ (i >> 2)) & 1) * 4) + ((i >> 2) & 1) * 2 + (i >> 3)
    for i in range(16)
]


def product(left, right, left_dim, right_dim):
    return lax.dot_general(
        left, right, (((left_dim,), (right_dim,)), ((), ())), preferred_element_type=F32
    )


def normalise(block):
    wide = block.astype(F32)
    return (wide * lax.rsqrt(jnp.mean(wide * wide, axis=-1, keepdims=True) + 1e-06)).astype(BF16)


def send_kernel(inputs_ref, cot_ref, first_ref, sent_ref):
    places, _, groups, tile, width = sent_ref.shape

    def part(block):
        return block.reshape(places, groups, -1, width)

    mixes, weights = [], []
    for a in range(inputs_ref.shape[1]):
        normed = normalise(inputs_ref[0, a])
        weights.append(part(cot_ref[0, a].astype(F32) * normed.astype(F32)))
        mixes.append(part(product(first_ref[a], normed, 1, 0)))
    for k, parts in enumerate((mixes, weights)):
        sent_ref[:, k] = jnp.concatenate(parts, axis=2).astype(BF16)


def build_sent(inputs, cotangent, first_blocks, places):
    _, rows, block, width = inputs.shape
    groups, step = 2, 2
    tile = step * block // places // groups
    whole = pl.BlockSpec((1, step, block, width), lambda a: (0, a, 0, 0))
    return pl.pallas_call(
        send_kernel,
        grid=(rows // step,),
        in_specs=[whole, whole, pl.BlockSpec((step, block, block), lambda a: (a, 0, 0))],
        out_specs=pl.BlockSpec((places, 2, groups, tile, width), lambda a: (0, 0, 0, a, 0)),
        out_shape=jax.ShapeDtypeStruct((places, 2, groups, tile * rows // step, width), BF16),
        compiler_params=pltpu.CompilerParams(vmem_limit_bytes=VMEM_LIMIT),
        name="send",
    )(inputs, cotangent, first_blocks)


def mlp_kernel(inputs_ref, cot_ref, up_ref, down_ref, up_t_ref, down_t_ref, normed_ref, cot_t_ref):
    @pl.when(pl.program_id(0) == 0)
    def _():
        normed_ref[...] = normalise(inputs_ref[...])
        cot_t_ref[...] = cot_ref[...].T

    field = product(normed_ref[...], up_ref[...], 1, 0)
    back = product(cot_ref[...], down_ref[...], 1, 1)
    scale, cubic = 0.7978845608028654, 0.044715
    square = field * field
    bend = jnp.tanh(scale * field * (1.0 + cubic * square))
    upper = 0.5 + 0.5 * bend
    hidden = (field * upper).astype(BF16)
    slope = upper + (0.5 * scale) * field * (1.0 - bend * bend) * (1.0 + 3.0 * cubic * square)
    up_slope = (back * slope).astype(BF16)
    down_t_ref[...] = product(cot_t_ref[...], hidden, 1, 0).astype(BF16)
    up_t_ref[...] = product(up_slope, normed_ref[...], 0, 0).astype(BF16)


def mlp_grads(inputs, cotangent, up_weight, down_weight):
    positions, width = inputs.shape
    units = up_weight.shape[1]
    step = 256
    whole = pl.BlockSpec((positions, width), lambda f: (0, 0))
    by_row = pl.BlockSpec((step, width), lambda f: (f, 0))
    by_col = pl.BlockSpec((width, step), lambda f: (0, f))
    return pl.pallas_call(
        mlp_kernel,
        grid=(units // step,),
        in_specs=[whole, whole, by_col, by_row],
        out_specs=[by_row, by_col],
        out_shape=[
            jax.ShapeDtypeStruct((units, width), BF16),
            jax.ShapeDtypeStruct((width, units), BF16),
        ],
        scratch_shapes=[pltpu.VMEM((positions, width), BF16), pltpu.VMEM((width, positions), BF16)],
        compiler_params=pltpu.CompilerParams(vmem_limit_bytes=VMEM_LIMIT),
        name="mlp",
    )(inputs, cotangent, up_weight, down_weight)


def value_half(both_ref, weighted_ref, weight_ref, out_ref):
    slopes = []
    groups = weighted_ref.shape[2]
    positions = both_ref.shape[0] // groups
    for k in range(groups):
        mixed = product(both_ref[pl.ds(k * positions, positions)], weight_ref[...], 1, 0)
        sigmoid_part = jax.nn.sigmoid(mixed)
        weighted = weighted_ref[:, 0, k].reshape(mixed.shape).astype(F32)
        slope = weighted * (sigmoid_part * (1.0 + mixed * (1.0 - sigmoid_part)))
        slopes.append(slope.astype(BF16))
    grad = product(jnp.concatenate(slopes, axis=0), both_ref[...], 0, 0).astype(BF16)
    size = grad.shape[0] // CHIPS
    pieces = [PIECE[2 * chip] % CHIPS for chip in range(CHIPS)]
    out_ref[...] = jnp.concatenate([grad[p * size : (p + 1) * size] for p in pieces], axis=0)


def mix_kernel(mix_ref, stacked_ref, both_ref):
    groups, positions, size = stacked_ref.shape
    blocks = positions // size
    take = lax.broadcasted_iota(jnp.int32, (size, positions), 1) // blocks
    spread = (take == lax.broadcasted_iota(jnp.int32, (size, positions), 0)).astype(BF16)
    row = lax.broadcasted_iota(jnp.int32, (positions, positions), 0)
    col = lax.broadcasted_iota(jnp.int32, (positions, positions), 1)
    same = row % blocks == col % blocks
    for k in range(groups):
        wide = product(stacked_ref[k], spread, 1, 0)
        second = jnp.where(same, wide, 0.0).astype(BF16)
        first_mix = mix_ref[:, 0, k].reshape(positions, -1)
        both_ref[pl.ds(k * positions, positions)] = product(second, first_mix, 1, 0).astype(BF16)


def half_kernel(part_ref, both_ref, weighted_ref, weight_ref, out_ref):
    value_half(both_ref, weighted_ref, weight_ref, out_ref)


def second_mix(came, second_blocks):
    places, _, groups, tile, width = came.shape
    size = second_blocks.shape[1]
    stacked = second_blocks.reshape(groups, -1, size, size).transpose(0, 2, 1, 3)
    stacked = stacked.reshape(groups, -1, size)
    return pl.pallas_call(
        mix_kernel,
        grid=(1,),
        in_specs=[
            pl.BlockSpec((places, 1, groups, tile, width), lambda k: (0, 0, 0, 0, 0)),
            pl.BlockSpec(stacked.shape, lambda k: (0, 0, 0)),
        ],
        out_specs=pl.BlockSpec((places * groups * tile, width), lambda k: (0, 0)),
        out_shape=jax.ShapeDtypeStruct((places * groups * tile, width), BF16),
        compiler_params=pltpu.CompilerParams(vmem_limit_bytes=SMALL_LIMIT),
        name="mix",
    )(came, stacked)


def value_part(part, both, came, value_weight):
    places, _, groups, tile, width = came.shape
    half = width // 2
    return pl.pallas_call(
        half_kernel,
        grid_spec=pltpu.PrefetchScalarGridSpec(
            num_scalar_prefetch=1,
            grid=(1,),
            in_specs=[
                pl.BlockSpec(both.shape, lambda k, p: (0, 0)),
                pl.BlockSpec((places, 1, groups, tile, half), lambda k, p: (0, 1, 0, 0, p[0])),
                pl.BlockSpec((width, half), lambda k, p: (0, p[0])),
            ],
            out_specs=pl.BlockSpec((half, width), lambda k, p: (0, 0)),
        ),
        out_shape=jax.ShapeDtypeStruct((half, width), BF16),
        compiler_params=pltpu.CompilerParams(vmem_limit_bytes=SMALL_LIMIT),
        name="half",
    )(part, both, came, value_weight)


def join_kernel(pieces_ref, value_ref, up_ref, down_ref, rows_ref):
    places, size, lanes = pieces_ref.shape
    for i in range(places):
        rows_ref[PIECE[i] * size : (PIECE[i] + 1) * size, :lanes] = pieces_ref[i]
    turned = rows_ref[...].T
    width = value_ref.shape[1]
    share = value_ref.shape[0]
    value_ref[...] = turned[:share]
    up_ref[:, :width] = turned[share : 2 * share]
    up_ref[:, width:] = turned[2 * share : 3 * share]
    down_ref[...] = turned[3 * share : 5 * share]


def join(pieces):
    places, size, lanes = pieces.shape
    width = places * size
    share = lanes // 5
    padded = -(-lanes // 128) * 128
    return pl.pallas_call(
        join_kernel,
        out_shape=[
            jax.ShapeDtypeStruct((share, width), BF16),
            jax.ShapeDtypeStruct((share, 2 * width), BF16),
            jax.ShapeDtypeStruct((2 * share, width), BF16),
        ],
        scratch_shapes=[pltpu.VMEM((width, padded), BF16)],
        compiler_params=pltpu.CompilerParams(vmem_limit_bytes=SMALL_LIMIT),
        name="join",
    )(pieces)


def swap(block, flip, over):
    return lax.ppermute(block, over, [(i, i ^ flip) for i in range(16)])


def add_swapped(keep, give, flip, over="dp"):
    return keep.astype(F32) + swap(give.astype(BF16), flip, over).astype(F32)


def halve(total, axis, bit, flip, over="dp"):
    keep = lax.dynamic_slice_in_dim(total, bit, 1, axis)
    give = lax.dynamic_slice_in_dim(total, 1 - bit, 1, axis)
    return add_swapped(keep, give, flip, over)


def scatter_chips(left, right):
    i = lax.axis_index("dp")
    x0, x1, y_hi = (i >> 1) & 1, (i >> 2) & 1, i >> 3
    out = []
    for straight, block in ((True, left), (False, right)):
        groups, rows, lanes = block.shape
        total = block.reshape(groups, 2, 2, 2, rows // 8, lanes)
        if straight:
            total = halve(total, 1, x0 ^ x1, 2)
            total = halve(total, 2, x1, 6)
        else:
            total = halve(total, 2, x1, 6)
            total = halve(total, 1, x0 ^ x1, 2)
        total = halve(total, 3, y_hi, 8)
        out.append(total.reshape(groups, rows // 8, lanes).astype(BF16))
    return out


def exchange(block, axis, groups=None):
    return lax.all_to_all(
        block, axis, split_axis=0, concat_axis=0, tiled=True, axis_index_groups=groups
    )


def same_core():
    return [[2 * chip + core for chip in range(CHIPS)] for core in range(2)]


def by_place(block, places):
    rows, lanes = block.shape
    return block.reshape(rows, places, lanes // places).transpose(1, 0, 2)


def local(inputs, cotangent, value_weight, up_weight, down_weight, first_blocks, second_blocks):
    width = inputs.shape[3]
    half = width // 2
    places = lax.axis_size("seq")
    share = width // places
    core = lax.axis_index("dp") & 1
    core_arg = jnp.full((1,), core, jnp.int32)
    total_tokens = (
        inputs.shape[0] * inputs.shape[1] * inputs.shape[2] * lax.axis_size("dp") * places
    )
    factor = float(total_tokens) ** (-0.5)

    def pack(parts):
        return jnp.concatenate([by_place(part, places) for part in parts], axis=2)

    sent = build_sent(inputs, cotangent, first_blocks, places)
    sent, flat = lax.optimization_barrier((sent, inputs.reshape(-1, width)))
    came = exchange(sent, "seq")

    up_t, down_t = mlp_grads(flat, cotangent.reshape(-1, width), up_weight, down_weight)
    up_t = halve(up_t.reshape(2, 2, half, width), 1, core, 1).reshape(2, half, width)
    down_t = halve(down_t.reshape(1, 2, half, 2 * width), 1, core, 1).reshape(1, half, 2 * width)
    up_t, down_t = scatter_chips(up_t, down_t)


    came, up_t, down_t = lax.optimization_barrier((came, up_t, down_t))
    both = second_mix(came, second_blocks)
    value_give = value_part(1 - core_arg, both, came, value_weight)
    value_keep = value_part(core_arg, both, came, value_weight)
    value_t = add_swapped(value_keep, value_give, 1).astype(BF16)

    value_t, up_t, down_t = lax.optimization_barrier((value_t, up_t, down_t))
    value_t = exchange(value_t.reshape(CHIPS, -1, width), "dp", same_core())
    mlp_part = pack((up_t[0], up_t[1], down_t[0]))
    value_t = jnp.sum(value_t.astype(F32), axis=0).astype(BF16)

    part = exchange(jnp.concatenate([pack((value_t,)), mlp_part], axis=2), "seq")
    part = (jnp.sum(part.astype(F32), axis=0) * factor).astype(BF16)
    return tuple(join(exchange(jnp.broadcast_to(part[None], (16,) + part.shape), "dp")))


def solution(mesh):
    placed = (
        P("dp", "seq", None, None),
        P("dp", "seq", None, None),
        P(),
        P(),
        P(),
        P("seq", None, None),
        P("seq", None, None),
    )
    return jax.shard_map(
        local,
        mesh=mesh,
        in_specs=placed,
        out_specs=(P("seq", None), P("seq", None), P("seq", None)),
        check_vma=False,
    )
```

```python
import jax
import jax.numpy as jnp
from jax import lax
from jax.experimental import pallas as pl
from jax.experimental.pallas import tpu as pltpu
from jax.sharding import PartitionSpec as P

BF16 = jnp.bfloat16
F32 = jnp.float32
VMEM_LIMIT = 56 * 1024 * 1024
SMALL_LIMIT = 24 * 1024 * 1024
CHIPS = 8
PIECE = [
    (i & 1) * 8 + ((((i >> 1) ^ (i >> 2)) & 1) * 4) + ((i >> 2) & 1) * 2 + (i >> 3)
    for i in range(16)
]


def product(left, right, left_dim, right_dim):
    return lax.dot_general(
        left, right, (((left_dim,), (right_dim,)), ((), ())), preferred_element_type=F32
    )


def normalise(block):
    wide = block.astype(F32)
    return (wide * lax.rsqrt(jnp.mean(wide * wide, axis=-1, keepdims=True) + 1e-06)).astype(BF16)


def send_kernel(inputs_ref, cot_ref, first_ref, sent_ref):
    places, _, groups, tile, width = sent_ref.shape

    def part(block):
        return block.reshape(places, groups, -1, width)

    mixes, weights = [], []
    for a in range(inputs_ref.shape[1]):
        normed = normalise(inputs_ref[0, a])
        weights.append(part(cot_ref[0, a].astype(F32) * normed.astype(F32)))
        mixes.append(part(product(first_ref[a], normed, 1, 0)))
    for k, parts in enumerate((mixes, weights)):
        sent_ref[:, k] = jnp.concatenate(parts, axis=2).astype(BF16)


def build_sent(inputs, cotangent, first_blocks, places):
    _, rows, block, width = inputs.shape
    groups, step = 2, 2
    tile = step * block // places // groups
    whole = pl.BlockSpec((1, step, block, width), lambda a: (0, a, 0, 0))
    return pl.pallas_call(
        send_kernel,
        grid=(rows // step,),
        in_specs=[whole, whole, pl.BlockSpec((step, block, block), lambda a: (a, 0, 0))],
        out_specs=pl.BlockSpec((places, 2, groups, tile, width), lambda a: (0, 0, 0, a, 0)),
        out_shape=jax.ShapeDtypeStruct((places, 2, groups, tile * rows // step, width), BF16),
        compiler_params=pltpu.CompilerParams(vmem_limit_bytes=VMEM_LIMIT),
        name="send",
    )(inputs, cotangent, first_blocks)


def mlp_kernel(inputs_ref, cot_ref, up_ref, down_ref, up_t_ref, down_t_ref, normed_ref, cot_t_ref):
    @pl.when(pl.program_id(0) == 0)
    def _():
        normed_ref[...] = normalise(inputs_ref[...])
        cot_t_ref[...] = cot_ref[...].T

    field = product(normed_ref[...], up_ref[...], 1, 0)
    back = product(cot_ref[...], down_ref[...], 1, 1)
    scale, cubic = 0.7978845608028654, 0.044715
    square = field * field
    bend = jnp.tanh(scale * field * (1.0 + cubic * square))
    upper = 0.5 + 0.5 * bend
    hidden = (field * upper).astype(BF16)
    slope = upper + (0.5 * scale) * field * (1.0 - bend * bend) * (1.0 + 3.0 * cubic * square)
    up_slope = (back * slope).astype(BF16)
    down_t_ref[...] = product(cot_t_ref[...], hidden, 1, 0).astype(BF16)
    up_t_ref[...] = product(up_slope, normed_ref[...], 0, 0).astype(BF16)


def mlp_grads(inputs, cotangent, up_weight, down_weight):
    positions, width = inputs.shape
    units = up_weight.shape[1]
    step = 256
    whole = pl.BlockSpec((positions, width), lambda f: (0, 0))
    by_row = pl.BlockSpec((step, width), lambda f: (f, 0))
    by_col = pl.BlockSpec((width, step), lambda f: (0, f))
    return pl.pallas_call(
        mlp_kernel,
        grid=(units // step,),
        in_specs=[whole, whole, by_col, by_row],
        out_specs=[by_row, by_col],
        out_shape=[
            jax.ShapeDtypeStruct((units, width), BF16),
            jax.ShapeDtypeStruct((width, units), BF16),
        ],
        scratch_shapes=[pltpu.VMEM((positions, width), BF16), pltpu.VMEM((width, positions), BF16)],
        compiler_params=pltpu.CompilerParams(vmem_limit_bytes=VMEM_LIMIT),
        name="mlp",
    )(inputs, cotangent, up_weight, down_weight)


def value_half(both_ref, weighted_ref, weight_ref, out_ref):
    slopes = []
    groups = weighted_ref.shape[2]
    positions = both_ref.shape[0] // groups
    for k in range(groups):
        mixed = product(both_ref[pl.ds(k * positions, positions)], weight_ref[...], 1, 0)
        sigmoid_part = jax.nn.sigmoid(mixed)
        weighted = weighted_ref[:, 0, k].reshape(mixed.shape).astype(F32)
        slope = weighted * (sigmoid_part * (1.0 + mixed * (1.0 - sigmoid_part)))
        slopes.append(slope.astype(BF16))
    grad = product(jnp.concatenate(slopes, axis=0), both_ref[...], 0, 0).astype(BF16)
    size = grad.shape[0] // CHIPS
    pieces = [PIECE[2 * chip] % CHIPS for chip in range(CHIPS)]
    out_ref[...] = jnp.concatenate([grad[p * size : (p + 1) * size] for p in pieces], axis=0)


def mix_kernel(mix_ref, stacked_ref, both_ref):
    groups, positions, size = stacked_ref.shape
    blocks = positions // size
    take = lax.broadcasted_iota(jnp.int32, (size, positions), 1) // blocks
    spread = (take == lax.broadcasted_iota(jnp.int32, (size, positions), 0)).astype(BF16)
    row = lax.broadcasted_iota(jnp.int32, (positions, positions), 0)
    col = lax.broadcasted_iota(jnp.int32, (positions, positions), 1)
    same = row % blocks == col % blocks
    for k in range(groups):
        wide = product(stacked_ref[k], spread, 1, 0)
        second = jnp.where(same, wide, 0.0).astype(BF16)
        first_mix = mix_ref[:, 0, k].reshape(positions, -1)
        both_ref[pl.ds(k * positions, positions)] = product(second, first_mix, 1, 0).astype(BF16)


def half_kernel(part_ref, both_ref, weighted_ref, weight_ref, out_ref):
    value_half(both_ref, weighted_ref, weight_ref, out_ref)


def second_mix(came, second_blocks):
    places, _, groups, tile, width = came.shape
    size = second_blocks.shape[1]
    stacked = second_blocks.reshape(groups, -1, size, size).transpose(0, 2, 1, 3)
    stacked = stacked.reshape(groups, -1, size)
    return pl.pallas_call(
        mix_kernel,
        grid=(1,),
        in_specs=[
            pl.BlockSpec((places, 1, groups, tile, width), lambda k: (0, 0, 0, 0, 0)),
            pl.BlockSpec(stacked.shape, lambda k: (0, 0, 0)),
        ],
        out_specs=pl.BlockSpec((places * groups * tile, width), lambda k: (0, 0)),
        out_shape=jax.ShapeDtypeStruct((places * groups * tile, width), BF16),
        compiler_params=pltpu.CompilerParams(vmem_limit_bytes=SMALL_LIMIT),
        name="mix",
    )(came, stacked)


def value_part(part, both, came, value_weight):
    places, _, groups, tile, width = came.shape
    half = width // 2
    return pl.pallas_call(
        half_kernel,
        grid_spec=pltpu.PrefetchScalarGridSpec(
            num_scalar_prefetch=1,
            grid=(1,),
            in_specs=[
                pl.BlockSpec(both.shape, lambda k, p: (0, 0)),
                pl.BlockSpec((places, 1, groups, tile, half), lambda k, p: (0, 1, 0, 0, p[0])),
                pl.BlockSpec((width, half), lambda k, p: (0, p[0])),
            ],
            out_specs=pl.BlockSpec((half, width), lambda k, p: (0, 0)),
        ),
        out_shape=jax.ShapeDtypeStruct((half, width), BF16),
        compiler_params=pltpu.CompilerParams(vmem_limit_bytes=SMALL_LIMIT),
        name="half",
    )(part, both, came, value_weight)


def join_kernel(core_ref, own_ref, other_ref, value_ref, up_ref, down_ref, rows_ref):
    chips, size, lanes = own_ref.shape
    first = core_ref[0] == 0
    for chip in range(chips):
        own, other = own_ref[chip], other_ref[chip]
        low = PIECE[2 * chip] * size
        high = PIECE[2 * chip + 1] * size
        rows_ref[low : low + size, :lanes] = jnp.where(first, own, other)
        rows_ref[high : high + size, :lanes] = jnp.where(first, other, own)
    turned = rows_ref[...].T
    width = value_ref.shape[1]
    share = value_ref.shape[0]
    value_ref[...] = turned[:share]
    up_ref[:, :width] = turned[share : 2 * share]
    up_ref[:, width:] = turned[2 * share : 3 * share]
    down_ref[...] = turned[3 * share : 5 * share]


def join(core, own, other):
    chips, size, lanes = own.shape
    width = 2 * chips * size
    share = lanes // 5
    padded = -(-lanes // 128) * 128
    whole = pl.BlockSpec(memory_space=pltpu.VMEM)
    return pl.pallas_call(
        join_kernel,
        in_specs=[pl.BlockSpec(memory_space=pltpu.SMEM), whole, whole],
        out_shape=[
            jax.ShapeDtypeStruct((share, width), BF16),
            jax.ShapeDtypeStruct((share, 2 * width), BF16),
            jax.ShapeDtypeStruct((2 * share, width), BF16),
        ],
        scratch_shapes=[pltpu.VMEM((width, padded), BF16)],
        compiler_params=pltpu.CompilerParams(vmem_limit_bytes=SMALL_LIMIT),
        name="join",
    )(core, own, other)


def swap(block, flip, over):
    return lax.ppermute(block, over, [(i, i ^ flip) for i in range(16)])


def add_swapped(keep, give, flip, over="dp"):
    return keep.astype(F32) + swap(give.astype(BF16), flip, over).astype(F32)


def halve(total, axis, bit, flip, over="dp"):
    keep = lax.dynamic_slice_in_dim(total, bit, 1, axis)
    give = lax.dynamic_slice_in_dim(total, 1 - bit, 1, axis)
    return add_swapped(keep, give, flip, over)


def scatter_chips(left, right):
    i = lax.axis_index("dp")
    x0, x1, y_hi = (i >> 1) & 1, (i >> 2) & 1, i >> 3
    out = []
    for straight, block in ((True, left), (False, right)):
        groups, rows, lanes = block.shape
        total = block.reshape(groups, 2, 2, 2, rows // 8, lanes)
        if straight:
            total = halve(total, 1, x0 ^ x1, 2)
            total = halve(total, 2, x1, 6)
        else:
            total = halve(total, 2, x1, 6)
            total = halve(total, 1, x0 ^ x1, 2)
        total = halve(total, 3, y_hi, 8)
        out.append(total.reshape(groups, rows // 8, lanes).astype(BF16))
    return out


def exchange(block, axis, groups=None):
    return lax.all_to_all(
        block, axis, split_axis=0, concat_axis=0, tiled=True, axis_index_groups=groups
    )


def same_core():
    return [[2 * chip + core for chip in range(CHIPS)] for core in range(2)]


def by_place(block, places):
    rows, lanes = block.shape
    return block.reshape(rows, places, lanes // places).transpose(1, 0, 2)


def local(inputs, cotangent, value_weight, up_weight, down_weight, first_blocks, second_blocks):
    width = inputs.shape[3]
    half = width // 2
    places = lax.axis_size("seq")
    share = width // places
    core = lax.axis_index("dp") & 1
    core_arg = jnp.full((1,), core, jnp.int32)
    total_tokens = (
        inputs.shape[0] * inputs.shape[1] * inputs.shape[2] * lax.axis_size("dp") * places
    )
    factor = float(total_tokens) ** (-0.5)

    def pack(parts):
        return jnp.concatenate([by_place(part, places) for part in parts], axis=2)

    sent = build_sent(inputs, cotangent, first_blocks, places)
    sent, flat = lax.optimization_barrier((sent, inputs.reshape(-1, width)))
    came = exchange(sent, "seq")

    up_t, down_t = mlp_grads(flat, cotangent.reshape(-1, width), up_weight, down_weight)
    up_t = halve(up_t.reshape(2, 2, half, width), 1, core, 1).reshape(2, half, width)
    down_t = halve(down_t.reshape(1, 2, half, 2 * width), 1, core, 1).reshape(1, half, 2 * width)
    up_t, down_t = scatter_chips(up_t, down_t)


    came, up_t, down_t = lax.optimization_barrier((came, up_t, down_t))
    both = second_mix(came, second_blocks)
    value_give = value_part(1 - core_arg, both, came, value_weight)
    value_keep = value_part(core_arg, both, came, value_weight)
    value_t = add_swapped(value_keep, value_give, 1).astype(BF16)

    value_t, up_t, down_t = lax.optimization_barrier((value_t, up_t, down_t))
    value_t = exchange(value_t.reshape(CHIPS, -1, width), "dp", same_core())
    mlp_part = pack((up_t[0], up_t[1], down_t[0]))
    value_t = jnp.sum(value_t.astype(F32), axis=0).astype(BF16)

    part = exchange(jnp.concatenate([pack((value_t,)), mlp_part], axis=2), "seq")
    part = (jnp.sum(part.astype(F32), axis=0) * factor).astype(BF16)
    own = exchange(jnp.broadcast_to(part[None], (CHIPS,) + part.shape), "dp", same_core())
    return tuple(join(core_arg, own, swap(own, 1, "dp")))


def solution(mesh):
    placed = (
        P("dp", "seq", None, None),
        P("dp", "seq", None, None),
        P(),
        P(),
        P(),
        P("seq", None, None),
        P("seq", None, None),
    )
    return jax.shard_map(
        local,
        mesh=mesh,
        in_specs=placed,
        out_specs=(P("seq", None), P("seq", None), P("seq", None)),
        check_vma=False,
    )
```

```python
import jax
import jax.numpy as jnp
from jax import lax
from jax.experimental import pallas as pl
from jax.experimental.pallas import tpu as pltpu
from jax.sharding import PartitionSpec as P

BF16 = jnp.bfloat16
F32 = jnp.float32
VMEM_LIMIT = 56 * 1024 * 1024
SMALL_LIMIT = 24 * 1024 * 1024
CHIPS = 8
PIECE = [
    (i & 1) * 8 + ((((i >> 1) ^ (i >> 2)) & 1) * 4) + ((i >> 2) & 1) * 2 + (i >> 3)
    for i in range(16)
]


def product(left, right, left_dim, right_dim):
    return lax.dot_general(
        left, right, (((left_dim,), (right_dim,)), ((), ())), preferred_element_type=F32
    )


def normalise(block):
    wide = block.astype(F32)
    return (wide * lax.rsqrt(jnp.mean(wide * wide, axis=-1, keepdims=True) + 1e-06)).astype(BF16)


def send_kernel(inputs_ref, cot_ref, first_ref, sent_ref):
    places, _, groups, tile, width = sent_ref.shape

    def part(block):
        return block.reshape(places, groups, -1, width)

    mixes, weights = [], []
    for a in range(inputs_ref.shape[1]):
        normed = normalise(inputs_ref[0, a])
        weights.append(part(cot_ref[0, a].astype(F32) * normed.astype(F32)))
        mixes.append(part(product(first_ref[a], normed, 1, 0)))
    for k, parts in enumerate((mixes, weights)):
        sent_ref[:, k] = jnp.concatenate(parts, axis=2).astype(BF16)


def build_sent(inputs, cotangent, first_blocks, places):
    _, rows, block, width = inputs.shape
    groups, step = 2, 2
    tile = step * block // places // groups
    whole = pl.BlockSpec((1, step, block, width), lambda a: (0, a, 0, 0))
    return pl.pallas_call(
        send_kernel,
        grid=(rows // step,),
        in_specs=[whole, whole, pl.BlockSpec((step, block, block), lambda a: (a, 0, 0))],
        out_specs=pl.BlockSpec((places, 2, groups, tile, width), lambda a: (0, 0, 0, a, 0)),
        out_shape=jax.ShapeDtypeStruct((places, 2, groups, tile * rows // step, width), BF16),
        compiler_params=pltpu.CompilerParams(vmem_limit_bytes=VMEM_LIMIT),
        name="send",
    )(inputs, cotangent, first_blocks)


def mlp_kernel(inputs_ref, cot_ref, up_ref, down_ref, up_t_ref, down_t_ref, normed_ref, cot_t_ref):
    @pl.when(pl.program_id(0) == 0)
    def _():
        normed_ref[...] = normalise(inputs_ref[...])
        cot_t_ref[...] = cot_ref[...].T

    field = product(normed_ref[...], up_ref[...], 1, 0)
    back = product(cot_ref[...], down_ref[...], 1, 1)
    scale, cubic = 0.7978845608028654, 0.044715
    square = field * field
    bend = jnp.tanh(scale * field * (1.0 + cubic * square))
    upper = 0.5 + 0.5 * bend
    hidden = (field * upper).astype(BF16)
    slope = upper + (0.5 * scale) * field * (1.0 - bend * bend) * (1.0 + 3.0 * cubic * square)
    up_slope = (back * slope).astype(BF16)
    down_t_ref[...] = product(cot_t_ref[...], hidden, 1, 0).astype(BF16)
    up_t_ref[...] = product(up_slope, normed_ref[...], 0, 0).astype(BF16)


def mlp_grads(inputs, cotangent, up_weight, down_weight):
    positions, width = inputs.shape
    units = up_weight.shape[1]
    step = 256
    whole = pl.BlockSpec((positions, width), lambda f: (0, 0))
    by_row = pl.BlockSpec((step, width), lambda f: (f, 0))
    by_col = pl.BlockSpec((width, step), lambda f: (0, f))
    return pl.pallas_call(
        mlp_kernel,
        grid=(units // step,),
        in_specs=[whole, whole, by_col, by_row],
        out_specs=[by_row, by_col],
        out_shape=[
            jax.ShapeDtypeStruct((units, width), BF16),
            jax.ShapeDtypeStruct((width, units), BF16),
        ],
        scratch_shapes=[pltpu.VMEM((positions, width), BF16), pltpu.VMEM((width, positions), BF16)],
        compiler_params=pltpu.CompilerParams(vmem_limit_bytes=VMEM_LIMIT),
        name="mlp",
    )(inputs, cotangent, up_weight, down_weight)


def value_half(both_ref, weighted_ref, weight_ref, out_ref):
    groups = weighted_ref.shape[2]
    positions = both_ref.shape[0] // groups
    grad = None
    for k in range(groups):
        both = both_ref[pl.ds(k * positions, positions)]
        mixed = product(both, weight_ref[...], 1, 0)
        sigmoid_part = jax.nn.sigmoid(mixed)
        weighted = weighted_ref[:, 0, k].reshape(mixed.shape).astype(F32)
        slope = weighted * (sigmoid_part * (1.0 + mixed * (1.0 - sigmoid_part)))
        term = product(slope.astype(BF16), both, 0, 0)
        grad = term if grad is None else grad + term
    grad = grad.astype(BF16)
    size = grad.shape[0] // CHIPS
    pieces = [PIECE[2 * chip] % CHIPS for chip in range(CHIPS)]
    out_ref[...] = jnp.concatenate([grad[p * size : (p + 1) * size] for p in pieces], axis=0)


def mix_kernel(mix_ref, stacked_ref, both_ref):
    groups, positions, size = stacked_ref.shape
    blocks = positions // size
    take = lax.broadcasted_iota(jnp.int32, (size, positions), 1) // blocks
    spread = (take == lax.broadcasted_iota(jnp.int32, (size, positions), 0)).astype(BF16)
    row = lax.broadcasted_iota(jnp.int32, (positions, positions), 0)
    col = lax.broadcasted_iota(jnp.int32, (positions, positions), 1)
    same = row % blocks == col % blocks
    for k in range(groups):
        wide = product(stacked_ref[k], spread, 1, 0)
        second = jnp.where(same, wide, 0.0).astype(BF16)
        first_mix = mix_ref[:, 0, k].reshape(positions, -1)
        both_ref[pl.ds(k * positions, positions)] = product(second, first_mix, 1, 0).astype(BF16)


def half_kernel(part_ref, both_ref, weighted_ref, weight_ref, out_ref):
    value_half(both_ref, weighted_ref, weight_ref, out_ref)


def second_mix(came, second_blocks):
    places, _, groups, tile, width = came.shape
    size = second_blocks.shape[1]
    stacked = second_blocks.reshape(groups, -1, size, size).transpose(0, 2, 1, 3)
    stacked = stacked.reshape(groups, -1, size)
    return pl.pallas_call(
        mix_kernel,
        grid=(1,),
        in_specs=[
            pl.BlockSpec((places, 1, groups, tile, width), lambda k: (0, 0, 0, 0, 0)),
            pl.BlockSpec(stacked.shape, lambda k: (0, 0, 0)),
        ],
        out_specs=pl.BlockSpec((places * groups * tile, width), lambda k: (0, 0)),
        out_shape=jax.ShapeDtypeStruct((places * groups * tile, width), BF16),
        compiler_params=pltpu.CompilerParams(vmem_limit_bytes=SMALL_LIMIT),
        name="mix",
    )(came, stacked)


def value_part(part, both, came, value_weight):
    places, _, groups, tile, width = came.shape
    half = width // 2
    return pl.pallas_call(
        half_kernel,
        grid_spec=pltpu.PrefetchScalarGridSpec(
            num_scalar_prefetch=1,
            grid=(1,),
            in_specs=[
                pl.BlockSpec(both.shape, lambda k, p: (0, 0)),
                pl.BlockSpec((places, 1, groups, tile, half), lambda k, p: (0, 1, 0, 0, p[0])),
                pl.BlockSpec((width, half), lambda k, p: (0, p[0])),
            ],
            out_specs=pl.BlockSpec((half, width), lambda k, p: (0, 0)),
        ),
        out_shape=jax.ShapeDtypeStruct((half, width), BF16),
        compiler_params=pltpu.CompilerParams(vmem_limit_bytes=SMALL_LIMIT),
        name="half",
    )(part, both, came, value_weight)


def join_kernel(core_ref, own_ref, other_ref, value_ref, up_ref, down_ref, rows_ref):
    chips, size, lanes = own_ref.shape
    first = core_ref[0] == 0
    for chip in range(chips):
        own, other = own_ref[chip], other_ref[chip]
        low = PIECE[2 * chip] * size
        high = PIECE[2 * chip + 1] * size
        rows_ref[low : low + size, :lanes] = jnp.where(first, own, other)
        rows_ref[high : high + size, :lanes] = jnp.where(first, other, own)
    turned = rows_ref[...].T
    width = value_ref.shape[1]
    share = value_ref.shape[0]
    value_ref[...] = turned[:share]
    up_ref[:, :width] = turned[share : 2 * share]
    up_ref[:, width:] = turned[2 * share : 3 * share]
    down_ref[...] = turned[3 * share : 5 * share]


def join(core, own, other):
    chips, size, lanes = own.shape
    width = 2 * chips * size
    share = lanes // 5
    padded = -(-lanes // 128) * 128
    whole = pl.BlockSpec(memory_space=pltpu.VMEM)
    return pl.pallas_call(
        join_kernel,
        in_specs=[pl.BlockSpec(memory_space=pltpu.SMEM), whole, whole],
        out_shape=[
            jax.ShapeDtypeStruct((share, width), BF16),
            jax.ShapeDtypeStruct((share, 2 * width), BF16),
            jax.ShapeDtypeStruct((2 * share, width), BF16),
        ],
        scratch_shapes=[pltpu.VMEM((width, padded), BF16)],
        compiler_params=pltpu.CompilerParams(vmem_limit_bytes=SMALL_LIMIT),
        name="join",
    )(core, own, other)


def swap(block, flip, over):
    return lax.ppermute(block, over, [(i, i ^ flip) for i in range(16)])


def add_swapped(keep, give, flip, over="dp"):
    return keep.astype(F32) + swap(give.astype(BF16), flip, over).astype(F32)


def halve(total, axis, bit, flip, over="dp"):
    keep = lax.dynamic_slice_in_dim(total, bit, 1, axis)
    give = lax.dynamic_slice_in_dim(total, 1 - bit, 1, axis)
    return add_swapped(keep, give, flip, over)


def scatter_chips(left, right):
    i = lax.axis_index("dp")
    x0, x1, y_hi = (i >> 1) & 1, (i >> 2) & 1, i >> 3
    out = []
    for straight, block in ((True, left), (False, right)):
        groups, rows, lanes = block.shape
        total = block.reshape(groups, 2, 2, 2, rows // 8, lanes)
        if straight:
            total = halve(total, 1, x0 ^ x1, 2)
            total = halve(total, 2, x1, 6)
        else:
            total = halve(total, 2, x1, 6)
            total = halve(total, 1, x0 ^ x1, 2)
        total = halve(total, 3, y_hi, 8)
        out.append(total.reshape(groups, rows // 8, lanes).astype(BF16))
    return out


def exchange(block, axis, groups=None):
    return lax.all_to_all(
        block, axis, split_axis=0, concat_axis=0, tiled=True, axis_index_groups=groups
    )


def same_core():
    return [[2 * chip + core for chip in range(CHIPS)] for core in range(2)]


def by_place(block, places):
    rows, lanes = block.shape
    return block.reshape(rows, places, lanes // places).transpose(1, 0, 2)


def local(inputs, cotangent, value_weight, up_weight, down_weight, first_blocks, second_blocks):
    width = inputs.shape[3]
    half = width // 2
    places = lax.axis_size("seq")
    share = width // places
    core = lax.axis_index("dp") & 1
    core_arg = jnp.full((1,), core, jnp.int32)
    total_tokens = (
        inputs.shape[0] * inputs.shape[1] * inputs.shape[2] * lax.axis_size("dp") * places
    )
    factor = float(total_tokens) ** (-0.5)

    def pack(parts):
        return jnp.concatenate([by_place(part, places) for part in parts], axis=2)

    sent = build_sent(inputs, cotangent, first_blocks, places)
    sent, flat = lax.optimization_barrier((sent, inputs.reshape(-1, width)))
    came = exchange(sent, "seq")

    up_t, down_t = mlp_grads(flat, cotangent.reshape(-1, width), up_weight, down_weight)
    up_t = halve(up_t.reshape(2, 2, half, width), 1, core, 1).reshape(2, half, width)
    down_t = halve(down_t.reshape(1, 2, half, 2 * width), 1, core, 1).reshape(1, half, 2 * width)
    up_t, down_t = scatter_chips(up_t, down_t)


    came, up_t, down_t = lax.optimization_barrier((came, up_t, down_t))
    both = second_mix(came, second_blocks)
    value_give = value_part(1 - core_arg, both, came, value_weight)
    value_keep = value_part(core_arg, both, came, value_weight)
    value_t = add_swapped(value_keep, value_give, 1).astype(BF16)

    value_t, up_t, down_t = lax.optimization_barrier((value_t, up_t, down_t))
    value_t = exchange(value_t.reshape(CHIPS, -1, width), "dp", same_core())
    mlp_part = pack((up_t[0], up_t[1], down_t[0]))
    value_t = jnp.sum(value_t.astype(F32), axis=0).astype(BF16)

    part = exchange(jnp.concatenate([pack((value_t,)), mlp_part], axis=2), "seq")
    part = (jnp.sum(part.astype(F32), axis=0) * factor).astype(BF16)
    own = exchange(jnp.broadcast_to(part[None], (CHIPS,) + part.shape), "dp", same_core())
    return tuple(join(core_arg, own, swap(own, 1, "dp")))


def solution(mesh):
    placed = (
        P("dp", "seq", None, None),
        P("dp", "seq", None, None),
        P(),
        P(),
        P(),
        P("seq", None, None),
        P("seq", None, None),
    )
    return jax.shard_map(
        local,
        mesh=mesh,
        in_specs=placed,
        out_specs=(P("seq", None), P("seq", None), P("seq", None)),
        check_vma=False,
    )
```
